128 devices in a mesh: lon: 16 (over z, x_lo, core), lat: 8 (over y, x_hi).
Axes of the slice: x: 4 (x_hi: 2, x_lo: 2; x = x_hi * 2 + x_lo), y: 4, z: 4, core: 2. Of those that a mesh axis runs over, the one named last changes fastest.
Arguments:
- tokens: bfloat16 [96, 384, 4, 512], P('lat', 'lon'), may hold values from -6 to 6
- surface_kind: int32 [96, 384], P('lat', 'lon'), may hold values from 0 to 2
- kind_table: bfloat16 [3, 4, 512], replicated, may hold values from -3 to 3
- attn_q_w: bfloat16 [512, 512], replicated, as said below
- attn_kv_w: bfloat16 [512, 1024], replicated, as said below
- attn_out_w: bfloat16 [512, 512], replicated, may hold values from -0.25 to 0.25
- mlp_in_w: bfloat16 [512, 2048], replicated, may hold values from -0.25 to 0.25
- mlp_out_w: bfloat16 [2048, 512], replicated, may hold values from -0.125 to 0.125
- merge_w: bfloat16 [2048, 1024], replicated, may hold values from -0.125 to 0.125
- coarse_qkv_w: bfloat16 [1024, 3072], replicated
- coarse_out_w: bfloat16 [1024, 1024], replicated, may hold values from -0.1875 to 0.1875
Outputs:
- fine_state: bfloat16 [96, 384, 4, 512], P('lat', 'lon')
- coarse_state: bfloat16 [48, 192, 4, 1024], P('lat', 'lon')
The draws below stay inside these ranges and needn't reach their ends.
Inputs may be any that keep to these rules, and one draw needn't show every extreme that they name: `attn_q_w`: a projection of 512 inputs. `attn_kv_w`: a projection of 512 inputs.
All inputs are finite; a program needn't handle non-finite values.
Results may differ from the reference program's by a relative error of at most 0.02.
Values may be sent and summed in bfloat16 or wider, within the bound.
A program may use at most 128 MiB of HBM per device.

```python
import jax
import jax.numpy as jnp
from jax import lax

C1 = 512
C2 = 1024
H1 = 8
H2 = 16
HID = 2048
LEV = 4
KINDS = 3
NLAT = 96
NLON = 384


def draw_attn_q_w(key, part):
    key = jax.random.fold_in(key, 3)
    noise = jax.random.normal(key, (C1, C1), jnp.float32) * C1 ** (-0.5)
    return noise.astype(jnp.bfloat16)


def draw_attn_kv_w(key, part):
    key = jax.random.fold_in(key, 5)
    noise = jax.random.normal(key, (C1, 2 * C1), jnp.float32) * C1 ** (-0.5)
    return noise.astype(jnp.bfloat16)


def draw_coarse_qkv_w(key, part):
    key = jax.random.fold_in(key, 7)
    noise = jax.random.normal(key, (C2, 3 * C2), jnp.float32) * C2 ** (-0.5)
    return noise.astype(jnp.bfloat16)


def with_ends(values, own_key, least, high):
    longest = values.shape.index(max(values.shape))
    spots = []
    for shift in (0, 1):
        where = [jax.random.randint(jax.random.fold_in(own_key, axis), (), 0, length) for axis, length in enumerate(values.shape)]
        where[longest] = (where[longest] + shift) % values.shape[longest]
        spots.append(tuple(where))
    return values.at[spots[0]].set(least).at[spots[1]].set(high)


def level_of(stream_key, dims, split, smallest, largest):
    level = 1.0
    for position, shards_of in split:
        heights = jax.random.uniform(jax.random.fold_in(jax.random.fold_in(stream_key, 6), position), (shards_of,), jnp.float32, smallest / len(split), largest / len(split))
        level = level * jnp.repeat(jnp.exp(heights), dims[position] // shards_of).reshape((-1,) + (1,) * (len(dims) - 1 - position))
    return level


def bell_draw(own_key, extent, scale, limit, split=(), dtype=jnp.bfloat16):
    drawn = scale * jax.random.normal(own_key, extent, jnp.float32)
    if split:
        drawn = drawn * level_of(own_key, extent, split, -0.22, 0.18)
    return jnp.clip(drawn, -limit, limit).astype(dtype)


def setup_inputs(seed: int = 0) -> dict:
    keys = jax.random.split(jax.random.key(seed), 12)
    tokens = bell_draw(keys[0], (NLAT, NLON, LEV, C1), 1.0, 6.0, ((0, 8), (1, 16)))
    surface_kind = with_ends(jax.random.randint(keys[1], (NLAT, NLON), 0, KINDS), jax.random.fold_in(keys[1], 1), 0, KINDS - 1).astype(jnp.int32)
    kind_table = bell_draw(keys[2], (KINDS, LEV, C1), 0.5, 3.0)
    attn_q_w = draw_attn_q_w(jax.random.fold_in(keys[11], 71), 0)
    attn_kv_w = draw_attn_kv_w(jax.random.fold_in(keys[11], 71), 0)
    attn_out_w = bell_draw(keys[5], (C1, C1), C1 ** -0.5, 0.25)
    mlp_in_w = bell_draw(keys[6], (C1, HID), C1 ** -0.5, 0.25)
    mlp_out_w = bell_draw(keys[7], (HID, C1), HID ** -0.5, 0.125)
    merge_w = bell_draw(keys[8], (4 * C1, C2), (4 * C1) ** -0.5, 0.125)
    coarse_qkv_w = draw_coarse_qkv_w(jax.random.fold_in(keys[11], 71), 0)
    coarse_out_w = bell_draw(keys[10], (C2, C2), C2 ** -0.5, 0.1875)
    return {"tokens": tokens, "surface_kind": surface_kind, "kind_table": kind_table, "attn_q_w": attn_q_w, "attn_kv_w": attn_kv_w, "attn_out_w": attn_out_w, "mlp_in_w": mlp_in_w, "mlp_out_w": mlp_out_w, "merge_w": merge_w, "coarse_qkv_w": coarse_qkv_w, "coarse_out_w": coarse_out_w}


epsilon = 1e-05

def normalize(tensor):
    tensor = tensor.astype(jnp.float32)
    centred = tensor - lax.optimization_barrier(jnp.mean(tensor, axis=-1, keepdims=True))
    spread = lax.optimization_barrier(jnp.mean(centred * centred, axis=-1, keepdims=True))
    return (centred * lax.rsqrt(spread + epsilon)).astype(jnp.bfloat16)

def to_windows(tensor):
    lat_rows, lon_cols, levels, feat_width = tensor.shape
    tensor = tensor.reshape(lat_rows // 6, 6, lon_cols // 12, 12, levels // 2, 2, feat_width)
    tensor = tensor.transpose(0, 2, 4, 1, 3, 5, 6)
    return tensor.reshape(lat_rows // 6, lon_cols // 12 * (levels // 2), 144, feat_width)

def from_windows(tensor, lat_rows, lon_cols, levels):
    feat_width = tensor.shape[-1]
    tensor = tensor.reshape(lat_rows // 6, lon_cols // 12, levels // 2, 6, 12, 2, feat_width)
    tensor = tensor.transpose(0, 3, 1, 4, 2, 5, 6)
    return tensor.reshape(lat_rows, lon_cols, levels, feat_width)

def window_attention(queries, key_part, value_part, key_valid, head_count):
    lat_rows, lon_cols, levels, feat_width = queries.shape
    head_size = feat_width // head_count
    score_scale = head_size ** (-0.5)
    mask_all = to_windows(key_valid[..., None].astype(jnp.float32))[..., 0]

    def window_row(pieces):
        query_win, key_win, value_win, mask_win = pieces
        win_count = query_win.shape[0]
        query_heads = query_win.reshape(win_count, 144, head_count, head_size).astype(jnp.float32)
        key_heads = key_win.reshape(win_count, 144, head_count, head_size).astype(jnp.float32)
        value_heads = value_win.reshape(win_count, 144, head_count, head_size).astype(jnp.float32)
        scores = jnp.einsum('nqhd,nkhd->nhqk', query_heads, key_heads) * score_scale
        scores = jnp.where(mask_win[:, None, None, :] > 0.5, scores, -1e+30)
        row_top = lax.optimization_barrier(jnp.max(scores, axis=-1, keepdims=True))
        weights = jnp.exp(scores - row_top)
        weights_bf = (weights / lax.optimization_barrier(jnp.sum(weights, axis=-1, keepdims=True))).astype(jnp.bfloat16)
        mixture = jnp.einsum('nhqk,nkhd->nqhd', weights_bf.astype(jnp.float32), value_heads)
        return mixture.reshape(win_count, 144, feat_width).astype(jnp.bfloat16)
    result = lax.map(window_row, (to_windows(queries), to_windows(key_part), to_windows(value_part), mask_all))
    return from_windows(result, lat_rows, lon_cols, levels)

def shifted_attention(queries, key_part, value_part, head_count):
    lat_rows, lon_cols, levels, feat_width = queries.shape

    def framed(tensor):
        return jnp.pad(jnp.roll(tensor, 6, axis=1), ((3, 3), (0, 0), (1, 1), (0, 0)))
    key_valid = jnp.pad(jnp.ones((lat_rows, lon_cols, levels), bool), ((3, 3), (0, 0), (1, 1)))
    result = window_attention(framed(queries), framed(key_part), framed(value_part), key_valid, head_count)
    return jnp.roll(result[3:-3, :, 1:-1], -6, axis=1)

def merge_patches(grid_state):
    lat_rows, lon_cols, levels, feat_width = grid_state.shape
    grid_state = grid_state.reshape(lat_rows // 2, 2, lon_cols // 2, 2, levels, feat_width)
    grid_state = grid_state.transpose(0, 2, 4, 3, 1, 5)
    return grid_state.reshape(lat_rows // 2, lon_cols // 2, levels, 4 * feat_width)

def reference(tokens, surface_kind, kind_table, attn_q_w, attn_kv_w, attn_out_w, mlp_in_w, mlp_out_w, merge_w, coarse_qkv_w, coarse_out_w):
    onehot = (surface_kind[..., None] == jnp.arange(KINDS).astype(jnp.int32)).astype(jnp.float32)
    kind_embed = jnp.einsum('abk,klc->ablc', onehot, kind_table.astype(jnp.float32))
    embedded = (tokens.astype(jnp.float32) + kind_embed).astype(jnp.bfloat16)
    normed = normalize(embedded)
    queries = jnp.dot(normed, attn_q_w, preferred_element_type=jnp.float32).astype(jnp.bfloat16)
    key_value = jnp.dot(normed, attn_kv_w, preferred_element_type=jnp.float32).astype(jnp.bfloat16)
    attended = shifted_attention(queries, key_value[..., :C1], key_value[..., C1:], H1)
    after_attn = (embedded.astype(jnp.float32) + jnp.dot(attended, attn_out_w, preferred_element_type=jnp.float32)).astype(jnp.bfloat16)
    hidden = jax.nn.gelu(jnp.dot(normalize(after_attn), mlp_in_w, preferred_element_type=jnp.float32)).astype(jnp.bfloat16)
    fine_state = (after_attn.astype(jnp.float32) + jnp.dot(hidden, mlp_out_w, preferred_element_type=jnp.float32)).astype(jnp.bfloat16)
    merged = merge_patches(fine_state)
    coarse_in = jnp.dot(normalize(merged), merge_w, preferred_element_type=jnp.float32).astype(jnp.bfloat16)
    triple = jnp.dot(normalize(coarse_in), coarse_qkv_w, preferred_element_type=jnp.float32).astype(jnp.bfloat16)
    coarse_mix = shifted_attention(triple[..., :C2], triple[..., C2:2 * C2], triple[..., 2 * C2:], H2)
    coarse_state = (coarse_in.astype(jnp.float32) + jnp.dot(coarse_mix, coarse_out_w, preferred_element_type=jnp.float32)).astype(jnp.bfloat16)
    return (fine_state, coarse_state)
```

```python
import functools
import math

import jax
import jax.numpy as jnp
import numpy as np
from jax import lax
from jax.experimental import pallas as pl
from jax.experimental.pallas import tpu as pltpu
from jax.sharding import PartitionSpec as P

EPS = 1e-05
BR, BC, LEV = 3, 6, 4
ROWS = BR * BC * LEV
PAD = 80
WIN = 4 * ROWS
GRP = WIN // 2
HD = 64
F32 = jnp.float32
BF16 = jnp.bfloat16


def selections():
    out = np.zeros((6, 4 * PAD, 4 * PAD), np.float32)
    for b in range(4):
        for r in range(BR):
            for c in range(BC):
                for l in range(LEV):
                    i = b * PAD + (r * BC + c) * LEV + l
                    slab = (r * 4 * BC + b * BC + c) * LEV + l
                    out[0, i, slab] = 1
                    out[1, slab, i] = 1
                    g = 1 if l in (1, 2) else 0
                    li = (0, 0, 1, 1)[l]
                    win = g * GRP + li * (GRP // 2) + b * BR * BC + r * BC + c
                    out[2, win, i] = 1
                    out[3, i, win] = 1
                    rc = (((b // 2) * BR + r) * 2 * BC + (b % 2) * BC + c) * LEV + l
                    out[5, rc, i] = 1
    for k in range(4):
        for ci in range(BR):
            for cj in range(BC):
                for l in range(LEV):
                    fr, fc = 2 * ci + k % 2, 2 * cj + k // 2
                    b = (fr // BR) * 2 + fc // BC
                    i = b * PAD + ((fr % BR) * BC + fc % BC) * LEV + l
                    out[4, k * PAD + (ci * BC + cj) * LEV + l, i] = 1
    return out


def biases():
    at = np.arange(GRP)
    level = at // (GRP // 2)
    half = at % (GRP // 2) // (GRP // 4)
    same_level = level[:, None] == level[None, :]
    same_half = half[:, None] == half[None, :]
    ok = [same_level, np.ones_like(same_level), same_level & same_half, same_half]
    return np.where(np.stack(ok), 0.0, -1e30).astype(np.float32)


def norm(v):
    v = v.astype(F32)
    c = v - jnp.mean(v, axis=-1, keepdims=True)
    s = jnp.mean(c * c, axis=-1, keepdims=True)
    return (c * lax.rsqrt(s + EPS)).astype(BF16)


def mm(a, b):
    return jnp.dot(a, b, preferred_element_type=F32)


def attention(q, k, v, bias, first_bias, out, width):
    lane = lax.broadcasted_iota(jnp.int32, (GRP, 2 * HD), 1)
    low = lane < HD
    zero = jnp.zeros((GRP, 2 * HD), BF16)
    for g in range(2):
        rows = slice(g * GRP, (g + 1) * GRP)
        b = bias[first_bias + g]
        b = jnp.concatenate([b, b], axis=0)
        for pair in range(width // (2 * HD)):
            lanes = slice(pair * 2 * HD, (pair + 1) * 2 * HD)
            qp = q[rows, lanes]
            qq = jnp.concatenate([jnp.where(low, qp, zero), jnp.where(low, zero, qp)], axis=0)
            s = lax.dot_general(
                qq, k[rows, lanes], (((1,), (1,)), ((), ())), preferred_element_type=F32
            )
            s = s + b
            p = jnp.exp2(s - jnp.max(s, axis=-1, keepdims=True))
            total = jnp.sum(p, axis=-1, keepdims=True)
            o = mm(p.astype(BF16), v[rows, lanes]) / total
            out[rows, lanes] = jnp.where(low, o[:GRP], o[GRP:]).astype(BF16)


def kernel(
    n_lat, n_lon, x, code, table, sel_h, bias_h,
    wq_h, wkv_h, wo_h, w1_h, w2_h, wm_h, wc_h, wco_h,
    fine, coarse,
    sel, bias, wq, wkv, wo, w1, w2, wm, wc, wco,
    emb, fs, rt, rl, rd, q, k, v, att, aft,
    merged, cin, cq, ck, cv, catt, cs, cr,
    load_sem, s1, r1, s2, r2, s3, r3, s4, r4,
):
    lat, lon = lax.axis_index("lat"), lax.axis_index("lon")
    up, down = lax.rem(lat + n_lat - 1, n_lat), lax.rem(lat + 1, n_lat)
    left, right = lax.rem(lon + n_lon - 1, n_lon), lax.rem(lon + 1, n_lon)

    loads = {}
    for at, (name, src, dst) in enumerate([
        ("sel", sel_h, sel), ("wq", wq_h, wq), ("wkv", wkv_h, wkv), ("bias", bias_h, bias),
        ("wo", wo_h, wo), ("w1", w1_h, w1), ("w2", w2_h, w2), ("wm", wm_h, wm),
        ("wc", wc_h, wc), ("wco", wco_h, wco),
    ]):
        loads[name] = pltpu.make_async_copy(src, dst, load_sem.at[at])
        loads[name].start()

    places = [(up, lon), (lat, left), (up, left), (down, lon), (lat, right), (down, right)]
    barrier = pltpu.get_barrier_semaphore()
    for a, o in places:
        pl.semaphore_signal(
            barrier, inc=1, device_id={"lat": a, "lon": o}, device_id_type=pl.DeviceIdType.MESH
        )

    def send(src, dst, ssem, rsem, a, o):
        return pltpu.make_async_remote_copy(
            src_ref=src, dst_ref=dst, send_sem=ssem, recv_sem=rsem,
            device_id={"lat": a, "lon": o}, device_id_type=pl.DeviceIdType.MESH,
        )

    def shift_up(grid, ssem, rsem):
        return [
            send(grid.at[0, 0], grid.at[4, 4], ssem.at[0], rsem.at[0], up, left),
            send(grid.at[0, 1], grid.at[4, 1], ssem.at[1], rsem.at[1], up, lon),
            send(grid.at[0, pl.ds(2, 2)], grid.at[4, pl.ds(2, 2)], ssem.at[2], rsem.at[2], up, lon),
            send(grid.at[1, 0], grid.at[1, 4], ssem.at[3], rsem.at[3], lat, left),
            send(grid.at[pl.ds(2, 2), 0], grid.at[pl.ds(2, 2), 4], ssem.at[4], rsem.at[4], lat, left),
        ]

    loads["sel"].wait()
    ids = lax.broadcasted_iota(jnp.int32, (16, WIN), 0)
    for s in range(4):
        hot = (ids == code[s]).astype(F32).astype(BF16)
        kind = lax.dot_general(
            hot, table[...], (((0,), (0,)), ((), ())), preferred_element_type=F32
        )
        e = (x[s * WIN:(s + 1) * WIN].astype(F32) + kind).astype(BF16)
        e = mm(sel[0][:, :WIN], e).astype(BF16)
        for b in range(4):
            emb[s, b] = e[b * PAD:(b + 1) * PAD]

    pl.semaphore_wait(barrier, len(places))
    first = shift_up(emb, s1, r1)
    for at in (3, 4, 1, 2, 0):
        first[at].start()

    for name in ("wq", "wkv", "bias", "wo", "w1", "w2"):
        loads[name].wait()
    second = shift_up(fs, s2, r2)
    back = [
        send(fs.at[pl.ds(0, 2), 3], rl.at[pl.ds(0, 2)], s3.at[0], r3.at[0], lat, right),
        send(fs.at[2, 3], rl.at[2], s3.at[1], r3.at[1], lat, right),
        send(fs.at[3, pl.ds(0, 2)], rt.at[pl.ds(0, 2)], s3.at[2], r3.at[2], down, lon),
        send(fs.at[3, 2], rt.at[2], s3.at[3], r3.at[3], down, lon),
        send(fs.at[3, 3], rd, s3.at[4], r3.at[4], down, right),
    ]
    scale = math.log2(math.e) / math.sqrt(HD)

    def window(w, carry):
        wr, wc_ = w // 2, w % 2

        @pl.when(w == 1)
        def _():
            first[3].wait_recv()
            first[4].wait_recv()

        @pl.when(w == 2)
        def _():
            first[1].wait_recv()
            first[2].wait_recv()

        @pl.when(w == 3)
        def _():
            first[0].wait_recv()

        r0, c0 = 1 + 2 * wr, 1 + 2 * wc_
        blocks = [emb[r0, c0], emb[r0, c0 + 1], emb[r0 + 1, c0], emb[r0 + 1, c0 + 1]]
        e = mm(sel[2][:WIN], jnp.concatenate(blocks, axis=0))
        aft[...] = e.astype(BF16)
        n = norm(e)
        q[...] = (mm(n, wq[...]) * scale).astype(BF16)
        k[...] = mm(n, wkv[:, :512]).astype(BF16)
        v[...] = mm(n, wkv[:, 512:]).astype(BF16)
        wrapped = jnp.where((lat == n_lat - 1) & (wr == 1), 2, 0)
        attention(q, k, v, bias, wrapped, att, 512)
        a = (aft[...].astype(F32) + mm(att[...], wo[...])).astype(BF16)
        aft[...] = a
        n = norm(a)
        acc = a.astype(F32)
        for j in range(0, 2048, 512):
            h = jax.nn.gelu(mm(n, w1[:, j:j + 512])).astype(BF16)
            acc = acc + mm(h, w2[j:j + 512])
        f = mm(sel[3][:, :WIN], acc.astype(BF16)).astype(BF16)
        r0, c0 = 2 * wr, 2 * wc_
        for b in range(4):
            fs[r0 + b // 2, c0 + b % 2] = f[b * PAD:(b + 1) * PAD]

        @pl.when(w == 0)
        def _():
            second[0].start()
            second[1].start()
            second[3].start()

        @pl.when(w == 1)
        def _():
            second[2].start()
            back[0].start()

        @pl.when(w == 2)
        def _():
            second[4].start()
            back[2].start()

        @pl.when(w == 3)
        def _():
            back[1].start()
            back[3].start()
            back[4].start()

        return carry

    lax.fori_loop(0, 4, window, 0)

    def quadrant(w, carry):
        wr, wc_ = w // 2, w % 2

        @pl.when(w == 1)
        def _():
            second[3].wait_recv()
            second[4].wait_recv()

        @pl.when(w == 2)
        def _():
            second[1].wait_recv()
            second[2].wait_recv()

        @pl.when(w == 3)
        def _():
            second[0].wait_recv()

        r0, c0 = 1 + 2 * wr, 1 + 2 * wc_
        blocks = [fs[r0, c0], fs[r0, c0 + 1], fs[r0 + 1, c0], fs[r0 + 1, c0 + 1]]
        m = mm(sel[4], jnp.concatenate(blocks, axis=0))
        m = jnp.concatenate([m[j * PAD:(j + 1) * PAD] for j in range(4)], axis=1)
        merged[w] = norm(m)
        return carry

    lax.fori_loop(0, 4, quadrant, 0)

    loads["wm"].wait()
    m = jnp.concatenate([merged[j] for j in range(4)], axis=0)
    for j in range(0, 1024, 512):
        t = mm(m, wm[:, j:j + 512]).astype(BF16)
        cin[:, j:j + 512] = mm(sel[2][:WIN], t).astype(BF16)
    n = norm(cin[...])
    loads["wc"].wait()
    for j in range(0, 1024, 512):
        cq[:, j:j + 512] = (mm(n, wc[:, j:j + 512]) * scale).astype(BF16)
        ck[:, j:j + 512] = mm(n, wc[:, 1024 + j:1536 + j]).astype(BF16)
        cv[:, j:j + 512] = mm(n, wc[:, 2048 + j:2560 + j]).astype(BF16)
    attention(cq, ck, cv, bias, jnp.where(lat == n_lat - 1, 2, 0), catt, 1024)
    loads["wco"].wait()
    for j in range(0, 1024, 512):
        t = (cin[:, j:j + 512].astype(F32) + mm(catt[...], wco[:, j:j + 512])).astype(BF16)
        t = mm(sel[3][:, :WIN], t).astype(BF16)
        for b in range(4):
            cs[b, :, j:j + 512] = t[b * PAD:(b + 1) * PAD]
    third = [
        send(cs.at[1], cr.at[1], s4.at[0], r4.at[0], lat, right),
        send(cs.at[2], cr.at[2], s4.at[1], r4.at[1], down, lon),
        send(cs.at[3], cr.at[0], s4.at[2], r4.at[2], down, right),
    ]
    for copy in third:
        copy.start()

    for copy in back:
        copy.wait_recv()
    for s in range(4):
        if s == 0:
            blocks = [rd[...], rt[0], rt[1], rt[2]]
        else:
            blocks = [rl[s - 1], fs[s - 1, 0], fs[s - 1, 1], fs[s - 1, 2]]
        fine[s * WIN:(s + 1) * WIN] = mm(sel[1][:WIN], jnp.concatenate(blocks, axis=0)).astype(BF16)

    for copy in third:
        copy.wait_recv()
    blocks = [cr[0], cr[2], cr[1], cs[0]]
    coarse[...] = mm(sel[5][:WIN], jnp.concatenate(blocks, axis=0)).astype(BF16)
    for copy in first + second + back + third:
        copy.wait_send()


def local(
    n_lat, n_lon, tokens, surface_kind, kind_table, attn_q_w, attn_kv_w, attn_out_w,
    mlp_in_w, mlp_out_w, merge_w, coarse_qkv_w, coarse_out_w,
):
    rows, cols, lev, width = tokens.shape
    x = tokens.reshape(rows * cols * lev, width)
    code = surface_kind[:, :, None] * lev + jnp.arange(lev, dtype=jnp.int32)
    code = code.reshape(4, 1, WIN)
    table = jnp.pad(kind_table.reshape(-1, width), ((0, 4), (0, 0)))
    sel = jnp.asarray(selections(), BF16)
    bias = jnp.asarray(biases())
    weights = [attn_q_w, attn_kv_w, attn_out_w, mlp_in_w, mlp_out_w, merge_w, coarse_qkv_w, coarse_out_w]
    vmem, hbm = pl.BlockSpec(memory_space=pltpu.VMEM), pl.BlockSpec(memory_space=pl.ANY)
    dma = pltpu.SemaphoreType.DMA
    buf = lambda *shape: pltpu.VMEM(shape, BF16)
    fine, coarse = pl.pallas_call(
        functools.partial(kernel, n_lat, n_lon),
        out_shape=(
            jax.ShapeDtypeStruct((4 * WIN, width), BF16),
            jax.ShapeDtypeStruct((WIN, 2 * width), BF16),
        ),
        in_specs=[vmem] * 3 + [hbm] * 10,
        out_specs=(vmem, vmem),
        scratch_shapes=[
            buf(*sel.shape), pltpu.VMEM(bias.shape, F32), *[buf(*w.shape) for w in weights],
            buf(5, 5, PAD, width), buf(5, 5, PAD, width),
            buf(3, PAD, width), buf(3, PAD, width), buf(PAD, width),
            *[buf(WIN, width)] * 5,
            buf(4, PAD, 4 * width), *[buf(WIN, 2 * width)] * 5,
            buf(4, PAD, 2 * width), buf(3, PAD, 2 * width),
            dma((10,)), dma((5,)), dma((5,)), dma((5,)), dma((5,)), dma((5,)), dma((5,)),
            dma((3,)), dma((3,)),
        ],
        compiler_params=pltpu.CompilerParams(
            collective_id=0, has_side_effects=True, vmem_limit_bytes=60 * 1024 * 1024
        ),
        name="block",
    )(x, code, table, sel, bias, *weights)
    return (
        fine.reshape(rows, cols, lev, width),
        coarse.reshape(rows // 2, cols // 2, lev, 2 * width),
    )


def solution(mesh):
    grid = P("lat", "lon", None, None)
    return jax.shard_map(
        functools.partial(local, mesh.shape["lat"], mesh.shape["lon"]),
        mesh=mesh,
        in_specs=(grid, P("lat", "lon")) + (P(),) * 9,
        out_specs=(grid, grid),
        check_vma=False,
    )
```

```python
import functools
import math

import jax
import jax.numpy as jnp
import numpy as np
from jax import lax
from jax.experimental import pallas as pl
from jax.experimental.pallas import tpu as pltpu
from jax.sharding import PartitionSpec as P

EPS = 1e-05
LEV = 4
WR, WC = 6, 12
SR, SC = WR // 2, WC // 2
WIN = WR * WC * LEV
GRP = WIN // 2
HD = 64
F32 = jnp.float32
BF16 = jnp.bfloat16


def orders():
    out = np.zeros((2, WIN, WIN), np.float32)
    for r in range(WR):
        for c in range(WC):
            for l in range(LEV):
                nat = (r * WC + c) * LEV + l
                g = 1 if l in (1, 2) else 0
                win = g * GRP + (l // 2) * (GRP // 2) + r * WC + c
                out[0, win, nat] = 1
                out[1, nat, win] = 1
    return out


def biases():
    at = np.arange(GRP)
    level = at // (GRP // 2)
    half = at % (GRP // 2) // (GRP // 4)
    same_level = level[:, None] == level[None, :]
    same_half = half[:, None] == half[None, :]
    ok = [same_level, np.ones_like(same_level), same_level & same_half, same_half]
    return np.where(np.stack(ok), 0.0, -1e30).astype(np.float32)


def norm(v):
    v = v.astype(F32)
    c = v - jnp.mean(v, axis=-1, keepdims=True)
    s = jnp.mean(c * c, axis=-1, keepdims=True)
    return (c * lax.rsqrt(s + EPS)).astype(BF16)


def mm(a, b):
    return jnp.dot(a, b, preferred_element_type=F32)


def attention(q, k, v, bias, first_bias, out, width):
    lane = lax.broadcasted_iota(jnp.int32, (GRP, 2 * HD), 1)
    low = lane < HD
    zero = jnp.zeros((GRP, 2 * HD), BF16)
    for g in range(2):
        rows = slice(g * GRP, (g + 1) * GRP)
        b = bias[first_bias + g]
        b = jnp.concatenate([b, b], axis=0)
        for pair in range(width // (2 * HD)):
            lanes = slice(pair * 2 * HD, (pair + 1) * 2 * HD)
            qp = q[rows, lanes]
            qq = jnp.concatenate([jnp.where(low, qp, zero), jnp.where(low, zero, qp)], axis=0)
            s = lax.dot_general(
                qq, k[rows, lanes], (((1,), (1,)), ((), ())), preferred_element_type=F32
            )
            s = s + b
            p = jnp.exp2(s - jnp.max(s, axis=-1, keepdims=True))
            total = jnp.sum(p, axis=-1, keepdims=True)
            o = mm(p.astype(BF16), v[rows, lanes]) / total
            out[rows, lanes] = jnp.where(low, o[:GRP], o[GRP:]).astype(BF16)


def kernel(
    n_lat, n_lon, x, kind, table, sel_h, bias_h,
    wq_h, wkv_h, wo_h, w1_h, w2_h, wm_h, wc_h, wco_h,
    fine, coarse,
    sel, bias, wq, wkv, wo, w1, w2, wm, wc, wco,
    emb, fs, q, k, v, att, aft, hid, cin, cq, ck, cv, catt, cs,
    load_sem, own_sem, s1, r1, s2, r2, s3, r3, s4, r4,
):
    lat, lon = lax.axis_index("lat"), lax.axis_index("lon")
    up, down = lax.rem(lat + n_lat - 1, n_lat), lax.rem(lat + 1, n_lat)
    left, right = lax.rem(lon + n_lon - 1, n_lon), lax.rem(lon + 1, n_lon)
    rows, cols = x.shape[0], x.shape[1]

    loads = {}
    for at, (name, src, dst) in enumerate([
        ("x", x, emb.at[pl.ds(0, rows), pl.ds(0, cols)]),
        ("sel", sel_h, sel), ("wq", wq_h, wq), ("wkv", wkv_h, wkv), ("bias", bias_h, bias),
        ("wo", wo_h, wo), ("w1", w1_h, w1), ("w2", w2_h, w2), ("wm", wm_h, wm),
        ("wc", wc_h, wc), ("wco", wco_h, wco),
    ]):
        loads[name] = pltpu.make_async_copy(src, dst, load_sem.at[at])
        loads[name].start()

    places = [(up, lon), (lat, left), (up, left), (down, lon), (lat, right), (down, right)]
    barrier = pltpu.get_barrier_semaphore()
    for a, o in places:
        pl.semaphore_signal(
            barrier, inc=1, device_id={"lat": a, "lon": o}, device_id_type=pl.DeviceIdType.MESH
        )

    def send(src, dst, ssem, rsem, a, o):
        return pltpu.make_async_remote_copy(
            src_ref=src, dst_ref=dst, send_sem=ssem, recv_sem=rsem,
            device_id={"lat": a, "lon": o}, device_id_type=pl.DeviceIdType.MESH,
        )

    def part(ref, r, c):
        return ref.at[pl.ds(r[0], r[1] - r[0]), pl.ds(c[0], c[1] - c[0])]

    def shift_up(grid, pieces, ssem, rsem):
        out = []
        for at, (r, c) in enumerate(pieces):
            a, o, rr, cc = lat, lon, r, c
            if r[1] <= SR:
                a, rr = up, (r[0] + rows, r[1] + rows)
            if c[1] <= SC:
                o, cc = left, (c[0] + cols, c[1] + cols)
            out.append(send(part(grid, r, c), part(grid, rr, cc), ssem.at[at], rsem.at[at], a, o))
        return out

    def shift_down(grid, place, pieces, n_rows, n_cols, ssem, rsem):
        out = []
        for at, (r, c) in enumerate(pieces):
            a, o = lat, lon
            rr, cc = (r[0] + SR, r[1] + SR), (c[0] + SC, c[1] + SC)
            if rr[0] >= n_rows:
                a, rr = down, (rr[0] - n_rows, rr[1] - n_rows)
            if cc[0] >= n_cols:
                o, cc = right, (cc[0] - n_cols, cc[1] - n_cols)
            out.append(send(part(grid, r, c), part(place, rr, cc), ssem.at[at], rsem.at[at], a, o))
        return out

    loads["x"].wait()
    kinds = kind[...].astype(F32)
    table_rows = jnp.concatenate([table[...], jnp.zeros_like(table[:1])], axis=0).reshape(16, -1)
    band = (SR, cols * LEV, cols)
    here = lax.broadcasted_iota(jnp.int32, band, 1) // LEV == lax.broadcasted_iota(jnp.int32, band, 2)
    n_tok = SR * cols * LEV
    lane = lax.broadcasted_iota(jnp.int32, (n_tok, 16), 1)
    level = lax.broadcasted_iota(jnp.int32, (n_tok, 16), 0) % LEV
    lane_level = (lane % LEV == level)
    lane_kind = (lane // LEV).astype(F32)
    for s in range(0, rows, SR):
        spread = jnp.broadcast_to(kinds[s:s + SR][:, None, :], band)
        own = jnp.sum(jnp.where(here, spread, 0.0), axis=-1, keepdims=True).reshape(n_tok, 1)
        hot = jnp.where(lane_level & (lane_kind == own), 1.0, 0.0).astype(BF16)
        e = emb[s:s + SR, :cols].reshape(n_tok, -1).astype(F32) + mm(hot, table_rows)
        emb[s:s + SR, :cols] = e.astype(BF16).reshape(SR, cols, LEV, -1)

    pl.semaphore_wait(barrier, len(places))
    first = shift_up(
        emb, [((3, 9), (0, 6)), ((0, 3), (6, 18)), ((0, 3), (0, 6)), ((0, 3), (18, 24)), ((9, 12), (0, 6))],
        s1, r1,
    )
    for copy in first:
        copy.start()
    second = shift_up(
        fs, [((0, 3), (0, 6)), ((0, 3), (6, 12)), ((3, 6), (0, 6)), ((0, 3), (12, 24)), ((6, 12), (0, 6))],
        s2, r2,
    )
    back = shift_down(
        fs, fine,
        [((0, 6), (18, 24)), ((9, 12), (0, 12)), ((6, 9), (18, 24)), ((9, 12), (12, 18)), ((9, 12), (18, 24))],
        rows, cols, s3, r3,
    )
    keep = pltpu.make_async_copy(
        part(fs, (0, rows - SR), (0, cols - SC)), part(fine, (SR, rows), (SC, cols)), own_sem.at[0]
    )
    scale = math.log2(math.e) / math.sqrt(HD)
    loads["sel"].wait()

    def window(w, carry):
        wr, wc_ = w // 2, w % 2

        @pl.when(w == 0)
        def _():
            for name in ("wq", "wkv", "bias"):
                loads[name].wait()

        @pl.when(w == 1)
        def _():
            first[0].wait_recv()

        @pl.when(w == 2)
        def _():
            first[1].wait_recv()

        @pl.when(w == 3)
        def _():
            for copy in first[2:]:
                copy.wait_recv()

        e = emb[pl.ds(SR + WR * wr, WR), pl.ds(SC + WC * wc_, WC)].reshape(WIN, -1)
        aft[...] = e
        n = mm(sel[0], norm(e)).astype(BF16)
        q[...] = (mm(n, wq[...]) * scale).astype(BF16)
        k[...] = mm(n, wkv[:, :512]).astype(BF16)
        v[...] = mm(n, wkv[:, 512:]).astype(BF16)
        wrapped = jnp.where((lat == n_lat - 1) & (wr == 1), 2, 0)
        attention(q, k, v, bias, wrapped, att, 512)

        @pl.when(w == 0)
        def _():
            for name in ("wo", "w1", "w2"):
                loads[name].wait()

        mixed = mm(sel[1], att[...]).astype(BF16)
        a = (aft[...].astype(F32) + mm(mixed, wo[...])).astype(BF16)
        aft[...] = a
        n = norm(a)
        for j in range(0, 2048, 512):
            hid[:, j:j + 512] = jax.nn.gelu(mm(n, w1[:, j:j + 512])).astype(BF16)
        f = (aft[...].astype(F32) + mm(hid[...], w2[...])).astype(BF16)
        fs[pl.ds(WR * wr, WR), pl.ds(WC * wc_, WC)] = f.reshape(WR, WC, LEV, -1)

        @pl.when(w == 0)
        def _():
            for copy in second[:3]:
                copy.start()

        @pl.when(w == 1)
        def _():
            second[3].start()
            back[0].start()

        @pl.when(w == 2)
        def _():
            second[4].start()
            back[1].start()

        @pl.when(w == 3)
        def _():
            for copy in back[2:]:
                copy.start()
            keep.start()

        return carry

    lax.fori_loop(0, 4, window, 0)

    loads["wm"].wait()
    for copy in second:
        copy.wait_recv()
    f = fs[pl.ds(SR, rows), pl.ds(SC, cols)].reshape(rows // 2, 2, cols // 2, 2, LEV, -1)
    m = norm(jnp.concatenate([f[:, j % 2, :, j // 2].reshape(WIN, -1) for j in range(4)], axis=1))
    for j in range(0, 1024, 512):
        cin[:, j:j + 512] = mm(m, wm[:, j:j + 512]).astype(BF16)
    n = mm(sel[0], norm(cin[...])).astype(BF16)
    loads["wc"].wait()
    for j in range(0, 1024, 512):
        cq[:, j:j + 512] = (mm(n, wc[:, j:j + 512]) * scale).astype(BF16)
        ck[:, j:j + 512] = mm(n, wc[:, 1024 + j:1536 + j]).astype(BF16)
        cv[:, j:j + 512] = mm(n, wc[:, 2048 + j:2560 + j]).astype(BF16)
    attention(cq, ck, cv, bias, jnp.where(lat == n_lat - 1, 2, 0), catt, 1024)
    loads["wco"].wait()
    mixed = mm(sel[1], catt[...]).astype(BF16)
    for j in range(0, 1024, 512):
        t = (cin[:, j:j + 512].astype(F32) + mm(mixed, wco[:, j:j + 512])).astype(BF16)
        cs[:, :, :, j:j + 512] = t.reshape(WR, WC, LEV, -1)
    third = shift_down(
        cs, coarse, [((0, 3), (6, 12)), ((3, 6), (0, 6)), ((3, 6), (6, 12))], WR, WC, s4, r4
    )
    for copy in third:
        copy.start()
    keep_too = pltpu.make_async_copy(
        part(cs, (0, SR), (0, SC)), part(coarse, (SR, WR), (SC, WC)), own_sem.at[1]
    )
    keep_too.start()
    for copy in back + third:
        copy.wait_recv()
    keep.wait()
    keep_too.wait()
    for copy in first + second + back + third:
        copy.wait_send()


def local(
    n_lat, n_lon, tokens, surface_kind, kind_table, attn_q_w, attn_kv_w, attn_out_w,
    mlp_in_w, mlp_out_w, merge_w, coarse_qkv_w, coarse_out_w,
):
    rows, cols, lev, width = tokens.shape
    sel = jnp.asarray(orders(), BF16)
    bias = jnp.asarray(biases())
    weights = [attn_q_w, attn_kv_w, attn_out_w, mlp_in_w, mlp_out_w, merge_w, coarse_qkv_w, coarse_out_w]
    vmem, hbm = pl.BlockSpec(memory_space=pltpu.VMEM), pl.BlockSpec(memory_space=pl.ANY)
    dma = pltpu.SemaphoreType.DMA
    buf = lambda *shape: pltpu.VMEM(shape, BF16)
    frame = buf(rows + SR, cols + SC, lev, width)
    return pl.pallas_call(
        functools.partial(kernel, n_lat, n_lon),
        out_shape=(
            jax.ShapeDtypeStruct((rows, cols, lev, width), BF16),
            jax.ShapeDtypeStruct((rows // 2, cols // 2, lev, 2 * width), BF16),
        ),
        in_specs=[hbm, vmem, vmem] + [hbm] * 10,
        out_specs=(hbm, hbm),
        scratch_shapes=[
            buf(*sel.shape), pltpu.VMEM(bias.shape, F32), *[buf(*w.shape) for w in weights],
            frame, frame, *[buf(WIN, width)] * 5, buf(WIN, 4 * width), *[buf(WIN, 2 * width)] * 5,
            buf(WR, WC, lev, 2 * width),
            dma((11,)), dma((2,)), dma((5,)), dma((5,)), dma((5,)), dma((5,)), dma((5,)), dma((5,)),
            dma((3,)), dma((3,)),
        ],
        compiler_params=pltpu.CompilerParams(
            collective_id=0, has_side_effects=True, vmem_limit_bytes=60 * 1024 * 1024
        ),
        name="block",
    )(tokens, surface_kind, kind_table, sel, bias, *weights)


def solution(mesh):
    grid = P("lat", "lon", None, None)
    return jax.shard_map(
        functools.partial(local, mesh.shape["lat"], mesh.shape["lon"]),
        mesh=mesh,
        in_specs=(grid, P("lat", "lon")) + (P(),) * 9,
        out_specs=(grid, grid),
        check_vma=False,
    )
```

```python
import functools
import math

import jax
import jax.numpy as jnp
import numpy as np
from jax import lax
from jax.experimental import pallas as pl
from jax.experimental.pallas import tpu as pltpu
from jax.sharding import PartitionSpec as P

EPS = 1e-05
LEV = 4
WR, WC = 6, 12
SR, SC = WR // 2, WC // 2
WIN = WR * WC * LEV
GRP = WIN // 2
POS = WR * WC
QPAD = 40
GROUPS = ((0, 3), (1, 2))
HD = 64
LANES = 128
F32 = jnp.float32
BF16 = jnp.bfloat16


def biases():
    at = np.arange(GRP)
    level = at // POS
    half = at % POS // (POS // 2)
    same_level = level[:, None] == level[None, :]
    same_half = half[:, None] == half[None, :]
    ok = [same_level, np.ones_like(same_level), same_level & same_half, same_half]
    full = np.where(np.stack(ok), 0.0, -1e30).astype(np.float32)
    halves = np.zeros((4, 2, 2, QPAD, GRP), np.float32)
    halves[:, :, :, :POS // 2] = full.reshape(4, 2, 2, POS // 2, GRP).transpose(0, 2, 1, 3, 4)
    return full, halves.reshape(8, 2 * QPAD, GRP)


def norm(v):
    v = v.astype(F32)
    c = v - jnp.mean(v, axis=-1, keepdims=True)
    s = jnp.mean(c * c, axis=-1, keepdims=True)
    return c * lax.rsqrt(s + EPS)


def mm(a, b):
    return jnp.dot(a, b, preferred_element_type=F32)


def by_level(tokens, levels, start, count):
    rows = [pl.ds(start * LEV + l, count, stride=LEV) for l in levels]
    tiles = [jnp.concatenate([tokens[j, r] for r in rows], axis=0) for j in range(tokens.shape[0])]
    return jnp.concatenate([t.astype(BF16) for t in tiles], axis=1)


def split_tiles(tokens, v):
    for j in range(tokens.shape[0]):
        tokens[j, :v.shape[0]] = v[:, j * LANES:(j + 1) * LANES]


def gather(tokens, rows):
    return jnp.concatenate([tokens[j, rows].astype(BF16) for j in range(tokens.shape[0])], axis=1)


def attention(q, k, v, b, out, levels, start, step, used):
    count, width = q.shape
    low = lax.broadcasted_iota(jnp.int32, (count, 2 * HD), 1) < HD
    zero = jnp.zeros((count, 2 * HD), BF16)
    b = jnp.concatenate([b, b], axis=0)
    for pair in range(width // (2 * HD)):
        lanes = slice(pair * 2 * HD, (pair + 1) * 2 * HD)
        qp = q[:, lanes]
        qq = jnp.concatenate([jnp.where(low, qp, zero), jnp.where(low, zero, qp)], axis=0)
        s = lax.dot_general(
            qq, k[:, lanes], (((1,), (1,)), ((), ())), preferred_element_type=F32
        )
        s = s + b
        p = jnp.exp2(s - jnp.max(s, axis=-1, keepdims=True))
        total = jnp.sum(p, axis=-1, keepdims=True)
        o = mm(p.astype(BF16), v[:, lanes]) / total
        o = jnp.where(low, o[:count], o[count:])
        for i, l in enumerate(levels):
            out[pair, pl.ds(start * LEV + l, used, stride=LEV)] = o[i * step:i * step + used]


def kernel(
    n_lat, n_lon, x, kind, table, bias_h, cbias_h,
    wq_h, wkv_h, wo_h, w1_h, w2_h, wm_h, wc_h, wco_h,
    fine, coarse,
    bias, cbias, wq, wkv, wo, w1, w2, wm, wc, wco,
    emb, fs, q, k, v, nat, att, aft, hid, cin, cq, ck, cv, cnat, catt, cs,
    load_sem, own_sem, s1, r1, s2, r2, s3, r3, s4, r4,
):
    lat, lon = lax.axis_index("lat"), lax.axis_index("lon")
    up, down = lax.rem(lat + n_lat - 1, n_lat), lax.rem(lat + 1, n_lat)
    left, right = lax.rem(lon + n_lon - 1, n_lon), lax.rem(lon + 1, n_lon)
    rows, cols = x.shape[0], x.shape[1]

    loads = {}
    for at, (name, src, dst) in enumerate([
        ("x", x, emb.at[pl.ds(0, rows), pl.ds(0, cols)]),
        ("wq", wq_h, wq), ("wkv", wkv_h, wkv), ("bias", bias_h, bias),
        ("wo", wo_h, wo), ("w1", w1_h, w1), ("w2", w2_h, w2),
        ("wm", wm_h, wm), ("wc", wc_h, wc), ("cbias", cbias_h, cbias), ("wco", wco_h, wco),
    ]):
        loads[name] = pltpu.make_async_copy(src, dst, load_sem.at[at])

    def load(*names):
        for name in names:
            loads[name].start()

    def loaded(*names):
        for name in names:
            loads[name].wait()

    load("x", "wq", "wkv")
    places = [(up, lon), (lat, left), (up, left), (down, lon), (lat, right), (down, right)]
    barrier = pltpu.get_barrier_semaphore()
    for a, o in places:
        pl.semaphore_signal(
            barrier, inc=1, device_id={"lat": a, "lon": o}, device_id_type=pl.DeviceIdType.MESH
        )

    def send(src, dst, ssem, rsem, a, o):
        return pltpu.make_async_remote_copy(
            src_ref=src, dst_ref=dst, send_sem=ssem, recv_sem=rsem,
            device_id={"lat": a, "lon": o}, device_id_type=pl.DeviceIdType.MESH,
        )

    def part(ref, r, c):
        return ref.at[pl.ds(r[0], r[1] - r[0]), pl.ds(c[0], c[1] - c[0])]

    def shift_up(grid, pieces, ssem, rsem):
        out = []
        for at, (r, c) in enumerate(pieces):
            a, o, rr, cc = lat, lon, r, c
            if r[1] <= SR:
                a, rr = up, (r[0] + rows, r[1] + rows)
            if c[1] <= SC:
                o, cc = left, (c[0] + cols, c[1] + cols)
            out.append(send(part(grid, r, c), part(grid, rr, cc), ssem.at[at], rsem.at[at], a, o))
        return out

    def shift_down(grid, place, pieces, n_rows, n_cols, ssem, rsem):
        out = []
        for at, (r, c) in enumerate(pieces):
            a, o = lat, lon
            rr, cc = (r[0] + SR, r[1] + SR), (c[0] + SC, c[1] + SC)
            if rr[0] >= n_rows:
                a, rr = down, (rr[0] - n_rows, rr[1] - n_rows)
            if cc[0] >= n_cols:
                o, cc = right, (cc[0] - n_cols, cc[1] - n_cols)
            out.append(send(part(grid, r, c), part(place, rr, cc), ssem.at[at], rsem.at[at], a, o))
        return out

    loaded("x")
    load("bias", "wo", "w1", "w2")
    kinds = kind[...].astype(F32)
    table_rows = jnp.concatenate([table[...], jnp.zeros_like(table[:1])], axis=0).reshape(16, -1)
    band = (SR, cols * LEV, cols)
    here = lax.broadcasted_iota(jnp.int32, band, 1) // LEV == lax.broadcasted_iota(jnp.int32, band, 2)
    n_tok = SR * cols * LEV
    lane = lax.broadcasted_iota(jnp.int32, (n_tok, 16), 1)
    level = lax.broadcasted_iota(jnp.int32, (n_tok, 16), 0) % LEV
    lane_level = (lane % LEV == level)
    lane_kind = (lane // LEV).astype(F32)
    for s in range(0, rows, SR):
        spread = jnp.broadcast_to(kinds[s:s + SR][:, None, :], band)
        own = jnp.sum(jnp.where(here, spread, 0.0), axis=-1, keepdims=True).reshape(n_tok, 1)
        hot = jnp.where(lane_level & (lane_kind == own), 1.0, 0.0).astype(BF16)
        e = emb[s:s + SR, :cols].reshape(n_tok, -1).astype(F32) + mm(hot, table_rows)
        emb[s:s + SR, :cols] = e.astype(BF16).reshape(SR, cols, LEV, -1)

    pl.semaphore_wait(barrier, len(places))
    first = shift_up(
        emb, [((0, 3), (6, 18)), ((3, 9), (0, 6)), ((0, 3), (18, 24)), ((0, 3), (0, 6)), ((9, 12), (0, 6))],
        s1, r1,
    )
    for copy in first:
        copy.start()
    second = shift_up(
        fs, [((0, 3), (0, 6)), ((0, 3), (6, 12)), ((3, 6), (0, 6)), ((0, 3), (12, 24)), ((6, 12), (0, 6))],
        s2, r2,
    )
    back = shift_down(
        fs, fine,
        [((0, 6), (18, 24)), ((9, 12), (0, 12)), ((6, 9), (18, 24)), ((9, 12), (12, 18)), ((9, 12), (18, 24))],
        rows, cols, s3, r3,
    )
    keep = pltpu.make_async_copy(
        part(fs, (0, rows - SR), (0, cols - SC)), part(fine, (SR, rows), (SC, cols)), own_sem.at[0]
    )
    scale = math.log2(math.e) / math.sqrt(HD)
    loaded("wq", "wkv")

    def window(w, carry):
        wr, wc_ = w // 2, w % 2

        @pl.when(w == 1)
        def _():
            first[1].wait_recv()

        @pl.when(w == 2)
        def _():
            first[0].wait_recv()

        @pl.when(w == 3)
        def _():
            for copy in first[2:]:
                copy.wait_recv()

        e = emb[pl.ds(SR + WR * wr, WR), pl.ds(SC + WC * wc_, WC)].reshape(WIN, -1)
        aft[...] = e
        split_tiles(nat, norm(e))
        n = jnp.concatenate([by_level(nat, levels, 0, POS) for levels in GROUPS], axis=0)
        q[...] = (mm(n, wq[...]) * scale).astype(BF16)
        k[...] = mm(n, wkv[:, :512]).astype(BF16)
        v[...] = mm(n, wkv[:, 512:]).astype(BF16)
        wrapped = jnp.where((lat == n_lat - 1) & (wr == 1), 2, 0)

        @pl.when(w == 0)
        def _():
            loaded("bias")

        for g, levels in enumerate(GROUPS):
            at = pl.ds(g * GRP, GRP)
            attention(q.at[at], k.at[at], v.at[at], bias[wrapped + g], att, levels, 0, POS, POS)

        @pl.when(w == 0)
        def _():
            loaded("wo", "w1", "w2")
            load("wm", "wc", "cbias", "wco")

        a = (aft[...].astype(F32) + mm(gather(att, slice(None)), wo[...])).astype(BF16)
        aft[...] = a
        n = norm(a).astype(BF16)
        for j in range(0, 2048, 512):
            hid[:, j:j + 512] = jax.nn.gelu(mm(n, w1[:, j:j + 512])).astype(BF16)
        f = (aft[...].astype(F32) + mm(hid[...], w2[...])).astype(BF16)
        fs[pl.ds(WR * wr, WR), pl.ds(WC * wc_, WC)] = f.reshape(WR, WC, LEV, -1)

        @pl.when(w == 0)
        def _():
            for copy in second[:3]:
                copy.start()

        @pl.when(w == 1)
        def _():
            second[3].start()

        @pl.when(w == 2)
        def _():
            second[4].start()

        return carry

    lax.fori_loop(0, 4, window, 0)

    loaded("wm")
    for copy in second:
        copy.wait_recv()
    for copy in back:
        copy.start()
    keep.start()
    f = fs[pl.ds(SR, rows), pl.ds(SC, cols)].reshape(rows // 2, 2, cols // 2, 2, LEV, -1)
    m = norm(jnp.concatenate([f[:, j % 2, :, j // 2].reshape(WIN, -1) for j in range(4)], axis=1)).astype(BF16)
    for j in range(0, 1024, 512):
        cin[:, j:j + 512] = mm(m, wm[:, j:j + 512]).astype(BF16)
    split_tiles(cnat, norm(cin[...]))
    cnat[:, WIN:] = jnp.zeros_like(cnat[:, WIN:])
    nk = jnp.concatenate([by_level(cnat, levels, 0, POS) for levels in GROUPS], axis=0)
    nq = [by_level(cnat, levels, h * POS // 2, QPAD) for h in range(2) for levels in GROUPS]
    nq = jnp.concatenate(nq, axis=0)
    loaded("wc", "cbias", "wco")
    for j in range(0, 1024, 512):
        cq[:, j:j + 512] = (mm(nq, wc[:, j:j + 512]) * scale).astype(BF16)
        ck[:, j:j + 512] = mm(nk, wc[:, 1024 + j:1536 + j]).astype(BF16)
        cv[:, j:j + 512] = mm(nk, wc[:, 2048 + j:2560 + j]).astype(BF16)
    wrapped = jnp.where(lat == n_lat - 1, 4, 0)
    third = shift_down(
        cs, coarse, [((3, 6), (0, 6)), ((3, 6), (6, 12)), ((0, 3), (6, 12))], WR, WC, s4, r4
    )
    keep_too = pltpu.make_async_copy(
        part(cs, (0, SR), (0, SC)), part(coarse, (SR, WR), (SC, WC)), own_sem.at[1]
    )
    for half in (1, 0):
        for g, levels in enumerate(GROUPS):
            at = pl.ds((half * 2 + g) * 2 * QPAD, 2 * QPAD)
            keys = pl.ds(g * GRP, GRP)
            attention(
                cq.at[at], ck.at[keys], cv.at[keys], cbias[wrapped + g * 2 + half],
                catt, levels, half * POS // 2, QPAD, POS // 2,
            )
        mixed = gather(catt, slice(half * GRP, (half + 1) * GRP))
        at = slice(half * GRP, (half + 1) * GRP)
        for j in range(0, 1024, 512):
            t = (cin[at, j:j + 512].astype(F32) + mm(mixed, wco[:, j:j + 512])).astype(BF16)
            cs[half * SR:(half + 1) * SR, :, :, j:j + 512] = t.reshape(SR, WC, LEV, -1)
        if half == 1:
            third[0].start()
            third[1].start()
        else:
            third[2].start()
            keep_too.start()
    for copy in back + third:
        copy.wait_recv()
    keep.wait()
    keep_too.wait()
    for copy in first + second + back + third:
        copy.wait_send()


def local(
    n_lat, n_lon, tokens, surface_kind, kind_table, attn_q_w, attn_kv_w, attn_out_w,
    mlp_in_w, mlp_out_w, merge_w, coarse_qkv_w, coarse_out_w,
):
    rows, cols, lev, width = tokens.shape
    consts = [jnp.asarray(a) for a in biases()]
    weights = [attn_q_w, attn_kv_w, attn_out_w, mlp_in_w, mlp_out_w, merge_w, coarse_qkv_w, coarse_out_w]
    vmem, hbm = pl.BlockSpec(memory_space=pltpu.VMEM), pl.BlockSpec(memory_space=pl.ANY)
    dma = pltpu.SemaphoreType.DMA
    buf = lambda *shape: pltpu.VMEM(shape, BF16)
    frame = buf(rows + SR, cols + SC, lev, width)
    return pl.pallas_call(
        functools.partial(kernel, n_lat, n_lon),
        out_shape=(
            buf(rows, cols, lev, width),
            buf(rows // 2, cols // 2, lev, 2 * width),
        ),
        in_specs=[hbm, vmem, vmem] + [hbm] * 10,
        out_specs=(hbm, hbm),
        scratch_shapes=[
            *[pltpu.VMEM(a.shape, a.dtype) for a in consts + weights],
            frame, frame, *[buf(WIN, width)] * 3, *[pltpu.VMEM((width // LANES, WIN, LANES), F32)] * 2, buf(WIN, width),
            buf(WIN, 4 * width),
            buf(WIN, 2 * width), buf(8 * QPAD, 2 * width), buf(WIN, 2 * width), buf(WIN, 2 * width),
            pltpu.VMEM((2 * width // LANES, WIN + LEV * (2 * QPAD - POS), LANES), F32),
            pltpu.VMEM((2 * width // LANES, WIN, LANES), F32),
            buf(WR, WC, lev, 2 * width),
            dma((11,)), dma((2,)), dma((5,)), dma((5,)), dma((5,)), dma((5,)), dma((5,)), dma((5,)),
            dma((3,)), dma((3,)),
        ],
        compiler_params=pltpu.CompilerParams(
            collective_id=0, has_side_effects=True, vmem_limit_bytes=60 * 1024 * 1024
        ),
        name="block",
    )(tokens, surface_kind, kind_table, *consts, *weights)


def solution(mesh):
    grid = P("lat", "lon", None, None)
    return jax.shard_map(
        functools.partial(local, mesh.shape["lat"], mesh.shape["lon"]),
        mesh=mesh,
        in_specs=(grid, P("lat", "lon")) + (P(),) * 9,
        out_specs=(grid, grid),
        check_vma=False,
    )
```

```python
import functools
import math

import jax
import jax.numpy as jnp
import numpy as np
from jax import lax
from jax.experimental import pallas as pl
from jax.experimental.pallas import tpu as pltpu
from jax.sharding import PartitionSpec as P

EPS = 1e-05
LEV = 4
WR, WC = 6, 12
SR, SC = WR // 2, WC // 2
WIN = WR * WC * LEV
GRP = WIN // 2
POS = WR * WC
QPAD = 40
GROUPS = ((0, 3), (1, 2))
HD = 64
LANES = 128
F32 = jnp.float32
BF16 = jnp.bfloat16


def biases():
    at = np.arange(GRP)
    level = at // POS
    half = at % POS // (POS // 2)
    same_level = level[:, None] == level[None, :]
    same_half = half[:, None] == half[None, :]
    ok = [same_level, np.ones_like(same_level), same_level & same_half, same_half]
    full = np.where(np.stack(ok), 0.0, -1e30).astype(np.float32)
    halves = np.zeros((4, 2, 2, QPAD, GRP), np.float32)
    halves[:, :, :, :POS // 2] = full.reshape(4, 2, 2, POS // 2, GRP).transpose(0, 2, 1, 3, 4)
    return full, halves.reshape(8, 2 * QPAD, GRP)


def norm(v):
    v = v.astype(F32)
    c = v - jnp.mean(v, axis=-1, keepdims=True)
    s = jnp.mean(c * c, axis=-1, keepdims=True)
    return c * lax.rsqrt(s + EPS)


def gelu(x):
    inner = x * (math.sqrt(2 / math.pi) + math.sqrt(2 / math.pi) * 0.044715 * (x * x))
    return 0.5 * x * (1.0 + jnp.tanh(inner))


def mm(a, b):
    return jnp.dot(a, b, preferred_element_type=F32)


def by_level(tokens, levels, start, count):
    rows = [pl.ds(start * LEV + l, count, stride=LEV) for l in levels]
    tiles = [jnp.concatenate([tokens[j, r] for r in rows], axis=0) for j in range(tokens.shape[0])]
    return jnp.concatenate([t.astype(BF16) for t in tiles], axis=1)


def split_tiles(tokens, v):
    for j in range(tokens.shape[0]):
        tokens[j, :v.shape[0]] = v[:, j * LANES:(j + 1) * LANES]


def gather(tokens, rows):
    return jnp.concatenate([tokens[j, rows].astype(BF16) for j in range(tokens.shape[0])], axis=1)


def attention(q, k, v, b, out, levels, start, step, used):
    count, width = q.shape
    low = lax.broadcasted_iota(jnp.int32, (count, 2 * HD), 1) < HD
    zero = jnp.zeros((count, 2 * HD), BF16)
    b = jnp.concatenate([b, b], axis=0)
    for pair in range(width // (2 * HD)):
        lanes = slice(pair * 2 * HD, (pair + 1) * 2 * HD)
        qp = q[:, lanes]
        qq = jnp.concatenate([jnp.where(low, qp, zero), jnp.where(low, zero, qp)], axis=0)
        s = lax.dot_general(
            qq, k[:, lanes], (((1,), (1,)), ((), ())), preferred_element_type=F32
        )
        s = s + b
        p = jnp.exp2(s - jnp.max(s, axis=-1, keepdims=True))
        total = jnp.sum(p, axis=-1, keepdims=True)
        o = mm(p.astype(BF16), v[:, lanes]) / total
        o = jnp.where(low, o[:count], o[count:])
        for i, l in enumerate(levels):
            out[pair, pl.ds(start * LEV + l, used, stride=LEV)] = o[i * step:i * step + used]
        yield


def kernel(
    n_lat, n_lon, x, kind_h, table_h, bias_h, cbias_h,
    wq_h, wkv_h, wo_h, w1_h, w2_h, wm_h, wc_h, wco_h,
    fine, coarse,
    kind, table, bias, cbias, wq, wkv, wo, w1, w2, wm, wc, wco,
    emb, fs, q, k, v, nat, att, aft, done, hid, cin, cq, ck, cv, cnat, catt, cs,
    load_sem, own_sem, s1, r1, s2, r2, s3, r3, s4, r4,
):
    lat, lon = lax.axis_index("lat"), lax.axis_index("lon")
    up, down = lax.rem(lat + n_lat - 1, n_lat), lax.rem(lat + 1, n_lat)
    left, right = lax.rem(lon + n_lon - 1, n_lon), lax.rem(lon + 1, n_lon)
    rows, cols = x.shape[0], x.shape[1]

    places = [(up, lon), (lat, left), (up, left), (down, lon), (lat, right), (down, right)]
    barrier = pltpu.get_barrier_semaphore()
    for a, o in places:
        pl.semaphore_signal(
            barrier, inc=1, device_id={"lat": a, "lon": o}, device_id_type=pl.DeviceIdType.MESH
        )

    loads = {}
    for at, (name, src, dst) in enumerate([
        ("kind", kind_h, kind), ("table", table_h, table), ("x", x, emb.at[pl.ds(0, rows), pl.ds(0, cols)]),
        ("wq", wq_h, wq), ("wkv", wkv_h, wkv), ("bias", bias_h, bias),
        ("wo", wo_h, wo), ("w1", w1_h, w1), ("w2", w2_h, w2),
        ("wm", wm_h, wm), ("wc", wc_h, wc), ("cbias", cbias_h, cbias), ("wco", wco_h, wco),
    ]):
        loads[name] = pltpu.make_async_copy(src, dst, load_sem.at[at])

    def load(*names):
        for name in names:
            loads[name].start()

    def loaded(*names):
        for name in names:
            loads[name].wait()

    load("kind", "table", "x", "wq", "wkv")
    def send(src, dst, ssem, rsem, a, o):
        return pltpu.make_async_remote_copy(
            src_ref=src, dst_ref=dst, send_sem=ssem, recv_sem=rsem,
            device_id={"lat": a, "lon": o}, device_id_type=pl.DeviceIdType.MESH,
        )

    def part(ref, r, c):
        return ref.at[pl.ds(r[0], r[1] - r[0]), pl.ds(c[0], c[1] - c[0])]

    def shift_up(grid, pieces, ssem, rsem):
        out = []
        for at, (r, c) in enumerate(pieces):
            a, o, rr, cc = lat, lon, r, c
            if r[1] <= SR:
                a, rr = up, (r[0] + rows, r[1] + rows)
            if c[1] <= SC:
                o, cc = left, (c[0] + cols, c[1] + cols)
            out.append(send(part(grid, r, c), part(grid, rr, cc), ssem.at[at], rsem.at[at], a, o))
        return out

    def shift_down(grid, place, pieces, n_rows, n_cols, ssem, rsem):
        out = []
        for at, (r, c) in enumerate(pieces):
            a, o = lat, lon
            rr, cc = (r[0] + SR, r[1] + SR), (c[0] + SC, c[1] + SC)
            if rr[0] >= n_rows:
                a, rr = down, (rr[0] - n_rows, rr[1] - n_rows)
            if cc[0] >= n_cols:
                o, cc = right, (cc[0] - n_cols, cc[1] - n_cols)
            out.append(send(part(grid, r, c), part(place, rr, cc), ssem.at[at], rsem.at[at], a, o))
        return out

    first = shift_up(
        emb, [((0, 3), (6, 18)), ((3, 9), (0, 6)), ((0, 3), (18, 24)), ((0, 3), (0, 6)), ((9, 12), (0, 6))],
        s1, r1,
    )

    loaded("kind", "table", "x")
    load("bias", "wo", "w1", "w2")
    kinds = kind[...].astype(F32)
    table_rows = jnp.concatenate([table[...], jnp.zeros_like(table[:1])], axis=0).reshape(16, -1)
    band = (SR, cols * LEV, cols)
    here = lax.broadcasted_iota(jnp.int32, band, 1) // LEV == lax.broadcasted_iota(jnp.int32, band, 2)
    n_tok = SR * cols * LEV
    lane = lax.broadcasted_iota(jnp.int32, (n_tok, 16), 1)
    level = lax.broadcasted_iota(jnp.int32, (n_tok, 16), 0) % LEV
    lane_level = (lane % LEV == level)
    lane_kind = (lane // LEV).astype(F32)
    for s in range(0, rows, SR):
        spread = jnp.broadcast_to(kinds[s:s + SR][:, None, :], band)
        own = jnp.sum(jnp.where(here, spread, 0.0), axis=-1, keepdims=True).reshape(n_tok, 1)
        hot = jnp.where(lane_level & (lane_kind == own), 1.0, 0.0).astype(BF16)
        e = emb[s:s + SR, :cols].reshape(n_tok, -1).astype(F32) + mm(hot, table_rows)
        emb[s:s + SR, :cols] = e.astype(BF16).reshape(SR, cols, LEV, -1)
        if s == 0:
            pl.semaphore_wait(barrier, len(places))
            for at in (0, 2, 3):
                first[at].start()
    first[1].start()
    first[4].start()
    second = shift_up(
        fs, [((0, 3), (0, 6)), ((0, 3), (6, 12)), ((3, 6), (0, 6)), ((0, 3), (12, 24)), ((6, 12), (0, 6))],
        s2, r2,
    )
    back = shift_down(
        fs, fine,
        [((0, 6), (18, 24)), ((9, 12), (0, 12)), ((6, 9), (18, 24)), ((9, 12), (12, 18)), ((9, 12), (18, 24))],
        rows, cols, s3, r3,
    )
    keep = pltpu.make_async_copy(
        part(fs, (0, rows - SR), (0, cols - SC)), part(fine, (SR, rows), (SC, cols)), own_sem.at[0]
    )
    scale = math.log2(math.e) / math.sqrt(HD)
    loaded("wq", "wkv")

    def front(w):
        wr, wc_ = w // 2, w % 2
        e = emb[pl.ds(SR + WR * wr, WR), pl.ds(SC + WC * wc_, WC)].reshape(WIN, -1)
        aft[...] = e
        split_tiles(nat, norm(e))
        yield
        n = jnp.concatenate([by_level(nat, levels, 0, POS) for levels in GROUPS], axis=0)
        q[...] = (mm(n, wq[...]) * scale).astype(BF16)
        yield
        k[...] = mm(n, wkv[:, :512]).astype(BF16)
        yield
        v[...] = mm(n, wkv[:, 512:]).astype(BF16)
        yield
        wrapped = jnp.where((lat == n_lat - 1) & (wr == 1), 2, 0)
        for g, levels in enumerate(GROUPS):
            at = pl.ds(g * GRP, GRP)
            for _ in attention(q.at[at], k.at[at], v.at[at], bias[wrapped + g], att, levels, 0, POS, POS):
                yield
        a = (aft[...].astype(F32) + mm(gather(att, slice(None)), wo[...])).astype(BF16)
        yield
        done[...] = a

    def back_half(w):
        wr, wc_ = w // 2, w % 2
        n = norm(done[...]).astype(BF16)
        yield
        for j in range(0, 2048, 512):
            hid[:, j:j + 512] = gelu(mm(n, w1[:, j:j + 512])).astype(BF16)
            yield
        for j in range(0, 512, 256):
            f = (done[:, j:j + 256].astype(F32) + mm(hid[...], w2[:, j:j + 256])).astype(BF16)
            fs[pl.ds(WR * wr, WR), pl.ds(WC * wc_, WC), :, j:j + 256] = f.reshape(WR, WC, LEV, -1)
            yield

    def window(w, carry):
        for _ in back_half(w - 1):
            pass

        @pl.when(w == 1)
        def _():
            for copy in second[:3]:
                copy.start()
            first[1].wait_recv()

        @pl.when(w == 2)
        def _():
            second[3].start()
            first[0].wait_recv()

        @pl.when(w == 3)
        def _():
            second[4].start()
            back[0].start()
            back[1].start()
            for copy in first[2:]:
                copy.wait_recv()

        for _ in front(w):
            pass
        return carry

    loaded("bias", "wo")
    for _ in front(0):
        pass
    loaded("w1", "w2")
    load("wm", "wc", "cbias", "wco")
    lax.fori_loop(1, 4, window, 0)
    for _ in back_half(3):
        pass
    for copy in back[2:]:
        copy.start()
    keep.start()

    loaded("wm")
    for copy in second:
        copy.wait_recv()
    f = fs[pl.ds(SR, rows), pl.ds(SC, cols)].reshape(rows // 2, 2, cols // 2, 2, LEV, -1)
    m = norm(jnp.concatenate([f[:, j % 2, :, j // 2].reshape(WIN, -1) for j in range(4)], axis=1)).astype(BF16)
    for j in range(0, 1024, 512):
        cin[:, j:j + 512] = mm(m, wm[:, j:j + 512]).astype(BF16)
    split_tiles(cnat, norm(cin[...]))
    cnat[:, WIN:] = jnp.zeros_like(cnat[:, WIN:])
    nk = jnp.concatenate([by_level(cnat, levels, 0, POS) for levels in GROUPS], axis=0)
    loaded("wc", "cbias", "wco")
    for j in range(0, 1024, 512):
        ck[:, j:j + 512] = mm(nk, wc[:, 1024 + j:1536 + j]).astype(BF16)
        cv[:, j:j + 512] = mm(nk, wc[:, 2048 + j:2560 + j]).astype(BF16)
    wrapped = jnp.where(lat == n_lat - 1, 4, 0)
    third = shift_down(
        cs, coarse, [((3, 6), (0, 6)), ((3, 6), (6, 12)), ((0, 3), (6, 12))], WR, WC, s4, r4
    )
    keep_too = pltpu.make_async_copy(
        part(cs, (0, SR), (0, SC)), part(coarse, (SR, WR), (SC, WC)), own_sem.at[1]
    )
    for half in (1, 0):
        nq = [by_level(cnat, levels, half * POS // 2, QPAD) for levels in GROUPS]
        nq = jnp.concatenate(nq, axis=0)
        for j in range(0, 1024, 512):
            cq[:, j:j + 512] = (mm(nq, wc[:, j:j + 512]) * scale).astype(BF16)
        for g, levels in enumerate(GROUPS):
            at = pl.ds(g * 2 * QPAD, 2 * QPAD)
            keys = pl.ds(g * GRP, GRP)
            for _ in attention(
                cq.at[at], ck.at[keys], cv.at[keys], cbias[wrapped + g * 2 + half],
                catt, levels, half * POS // 2, QPAD, POS // 2,
            ):
                pass
        mixed = gather(catt, slice(half * GRP, (half + 1) * GRP))
        at = slice(half * GRP, (half + 1) * GRP)
        for j in range(0, 1024, 512):
            t = (cin[at, j:j + 512].astype(F32) + mm(mixed, wco[:, j:j + 512])).astype(BF16)
            cs[half * SR:(half + 1) * SR, :, :, j:j + 512] = t.reshape(SR, WC, LEV, -1)
        if half == 1:
            third[0].start()
            third[1].start()
        else:
            third[2].start()
            keep_too.start()
    for copy in back + third:
        copy.wait_recv()
    keep.wait()
    keep_too.wait()
    for copy in first + second + back + third:
        copy.wait_send()


def local(
    n_lat, n_lon, tokens, surface_kind, kind_table, attn_q_w, attn_kv_w, attn_out_w,
    mlp_in_w, mlp_out_w, merge_w, coarse_qkv_w, coarse_out_w,
):
    rows, cols, lev, width = tokens.shape
    consts = [jnp.asarray(a) for a in biases()]
    weights = [attn_q_w, attn_kv_w, attn_out_w, mlp_in_w, mlp_out_w, merge_w, coarse_qkv_w, coarse_out_w]
    hbm = pl.BlockSpec(memory_space=pl.ANY)
    dma = pltpu.SemaphoreType.DMA
    buf = lambda *shape: pltpu.VMEM(shape, BF16)
    frame = buf(rows + SR, cols + SC, lev, width)
    return pl.pallas_call(
        functools.partial(kernel, n_lat, n_lon),
        out_shape=(
            buf(rows, cols, lev, width),
            buf(rows // 2, cols // 2, lev, 2 * width),
        ),
        in_specs=[hbm] * 13,
        out_specs=(hbm, hbm),
        scratch_shapes=[
            *[pltpu.VMEM(a.shape, a.dtype) for a in [surface_kind, kind_table] + consts + weights],
            frame, frame, *[buf(WIN, width)] * 3, *[pltpu.VMEM((width // LANES, WIN, LANES), F32)] * 2,
            buf(WIN, width), buf(WIN, width),
            buf(WIN, 4 * width),
            buf(WIN, 2 * width), buf(4 * QPAD, 2 * width), buf(WIN, 2 * width), buf(WIN, 2 * width),
            pltpu.VMEM((2 * width // LANES, WIN + LEV * (2 * QPAD - POS), LANES), F32),
            pltpu.VMEM((2 * width // LANES, WIN, LANES), F32),
            buf(WR, WC, lev, 2 * width),
            dma((13,)), dma((2,)), dma((5,)), dma((5,)), dma((5,)), dma((5,)), dma((5,)), dma((5,)),
            dma((3,)), dma((3,)),
        ],
        compiler_params=pltpu.CompilerParams(
            collective_id=0, has_side_effects=True, vmem_limit_bytes=60 * 1024 * 1024
        ),
        name="block",
    )(tokens, surface_kind, kind_table, *consts, *weights)


def solution(mesh):
    grid = P("lat", "lon", None, None)
    return jax.shard_map(
        functools.partial(local, mesh.shape["lat"], mesh.shape["lon"]),
        mesh=mesh,
        in_specs=(grid, P("lat", "lon")) + (P(),) * 9,
        out_specs=(grid, grid),
        check_vma=False,
    )
```

```python
import functools
import math

import jax
import jax.numpy as jnp
import numpy as np
from jax import lax
from jax.experimental import pallas as pl
from jax.experimental.pallas import tpu as pltpu
from jax.sharding import PartitionSpec as P

EPS = 1e-05
LEV = 4
WR, WC = 6, 12
SR, SC = WR // 2, WC // 2
WIN = WR * WC * LEV
GRP = WIN // 2
POS = WR * WC
QPAD = 40
GROUPS = ((0, 3), (1, 2))
HD = 64
LANES = 128
F32 = jnp.float32
BF16 = jnp.bfloat16


def biases():
    at = np.arange(GRP)
    level = at // POS
    half = at % POS // (POS // 2)
    same_level = level[:, None] == level[None, :]
    same_half = half[:, None] == half[None, :]
    ok = [same_level, np.ones_like(same_level), same_level & same_half, same_half]
    full = np.where(np.stack(ok), 0.0, -1e30).astype(np.float32)
    halves = np.zeros((4, 2, 2, QPAD, GRP), np.float32)
    halves[:, :, :, :POS // 2] = full.reshape(4, 2, 2, POS // 2, GRP).transpose(0, 2, 1, 3, 4)
    return full, halves.reshape(8, 2 * QPAD, GRP)


def norm(v):
    v = v.astype(F32)
    c = v - jnp.mean(v, axis=-1, keepdims=True)
    s = jnp.mean(c * c, axis=-1, keepdims=True)
    return c * lax.rsqrt(s + EPS)


def gelu(x):
    inner = x * (math.sqrt(2 / math.pi) + math.sqrt(2 / math.pi) * 0.044715 * (x * x))
    return 0.5 * x * (1.0 + jnp.tanh(inner))


def mm(a, b):
    return jnp.dot(a, b, preferred_element_type=F32)


def by_level(tokens, levels, start, count):
    rows = [pl.ds(start * LEV + l, count, stride=LEV) for l in levels]
    tiles = [jnp.concatenate([tokens[j, r] for r in rows], axis=0) for j in range(tokens.shape[0])]
    return jnp.concatenate([t.astype(BF16) for t in tiles], axis=1)


def split_tiles(tokens, v):
    for j in range(tokens.shape[0]):
        tokens[j, :v.shape[0]] = v[:, j * LANES:(j + 1) * LANES]


def gather(tokens, rows):
    return jnp.concatenate([tokens[j, rows].astype(BF16) for j in range(tokens.shape[0])], axis=1)


def attention(q, k, v, b, out, levels, start, step, used):
    count, width = q.shape
    low = lax.broadcasted_iota(jnp.int32, (count, 2 * HD), 1) < HD
    zero = jnp.zeros((count, 2 * HD), BF16)
    b = jnp.concatenate([b, b], axis=0)
    for pair in range(width // (2 * HD)):
        lanes = slice(pair * 2 * HD, (pair + 1) * 2 * HD)
        qp = q[:, lanes]
        qq = jnp.concatenate([jnp.where(low, qp, zero), jnp.where(low, zero, qp)], axis=0)
        s = lax.dot_general(
            qq, k[:, lanes], (((1,), (1,)), ((), ())), preferred_element_type=F32
        )
        s = s + b
        p = jnp.exp2(s - jnp.max(s, axis=-1, keepdims=True))
        total = jnp.sum(p, axis=-1, keepdims=True)
        o = mm(p.astype(BF16), v[:, lanes]) / total
        o = jnp.where(low, o[:count], o[count:])
        for i, l in enumerate(levels):
            out[pair, pl.ds(start * LEV + l, used, stride=LEV)] = o[i * step:i * step + used]
        yield


def kernel(
    n_lat, n_lon, x, kind_h, table_h, bias_h, cbias_h,
    wq_h, wkv_h, wo_h, w1_h, w2_h, wm_h, wc_h, wco_h,
    fine, coarse,
    kind, table, bias, cbias, wq, wkv, wo, w1, w2, wm, wc, wco,
    emb, fs, q, k, v, nat, att, aft, done, hid, cin, cq, ck, cv, cnat, catt, cs,
    load_sem, own_sem, s1, r1, s2, r2, s3, r3, s4, r4,
):
    lat, lon = lax.axis_index("lat"), lax.axis_index("lon")
    up, down = lax.rem(lat + n_lat - 1, n_lat), lax.rem(lat + 1, n_lat)
    left, right = lax.rem(lon + n_lon - 1, n_lon), lax.rem(lon + 1, n_lon)
    rows, cols = x.shape[0], x.shape[1]

    places = [(down, lon), (lat, right), (down, right)]
    barrier = pltpu.get_barrier_semaphore()
    for a, o in places:
        pl.semaphore_signal(
            barrier, inc=1, device_id={"lat": a, "lon": o}, device_id_type=pl.DeviceIdType.MESH
        )

    loads = {}
    for at, (name, src, dst) in enumerate([
        ("kind", kind_h, kind), ("table", table_h, table), ("x", x, emb.at[pl.ds(0, rows), pl.ds(0, cols)]),
        ("wq", wq_h, wq), ("wkv", wkv_h, wkv), ("bias", bias_h, bias),
        ("wo", wo_h, wo), ("w1", w1_h, w1), ("w2", w2_h, w2),
        ("wm", wm_h, wm), ("wc", wc_h, wc), ("cbias", cbias_h, cbias), ("wco", wco_h, wco),
    ]):
        loads[name] = pltpu.make_async_copy(src, dst, load_sem.at[at])

    def load(*names):
        for name in names:
            loads[name].start()

    def loaded(*names):
        for name in names:
            loads[name].wait()

    load("kind", "table", "x", "wq", "wkv")
    def send(src, dst, ssem, rsem, a, o):
        return pltpu.make_async_remote_copy(
            src_ref=src, dst_ref=dst, send_sem=ssem, recv_sem=rsem,
            device_id={"lat": a, "lon": o}, device_id_type=pl.DeviceIdType.MESH,
        )

    def part(ref, r, c):
        return ref.at[pl.ds(r[0], r[1] - r[0]), pl.ds(c[0], c[1] - c[0])]

    def shift_up(grid, pieces, ssem, rsem):
        out = []
        for at, (r, c) in enumerate(pieces):
            a, o, rr, cc = lat, lon, r, c
            if r[1] <= SR:
                a, rr = up, (r[0] + rows, r[1] + rows)
            if c[1] <= SC:
                o, cc = left, (c[0] + cols, c[1] + cols)
            out.append(send(part(grid, r, c), part(grid, rr, cc), ssem.at[at], rsem.at[at], a, o))
        return out

    def shift_down(grid, place, pieces, n_rows, n_cols, ssem, rsem):
        out = []
        for at, (r, c) in enumerate(pieces):
            a, o = lat, lon
            rr, cc = (r[0] + SR, r[1] + SR), (c[0] + SC, c[1] + SC)
            if rr[0] >= n_rows:
                a, rr = down, (rr[0] - n_rows, rr[1] - n_rows)
            if cc[0] >= n_cols:
                o, cc = right, (cc[0] - n_cols, cc[1] - n_cols)
            out.append(send(part(grid, r, c), part(place, rr, cc), ssem.at[at], rsem.at[at], a, o))
        return out

    first = shift_up(
        emb, [((0, 3), (6, 18)), ((3, 9), (0, 6)), ((0, 3), (18, 24)), ((0, 3), (0, 6)), ((9, 12), (0, 6))],
        s1, r1,
    )

    loaded("kind", "table", "x")
    load("bias", "wo", "w1", "w2")
    kinds = kind[...].astype(F32)
    table_rows = jnp.concatenate([table[...], jnp.zeros_like(table[:1])], axis=0).reshape(16, -1)
    band = (SR, cols * LEV, cols)
    here = lax.broadcasted_iota(jnp.int32, band, 1) // LEV == lax.broadcasted_iota(jnp.int32, band, 2)
    n_tok = SR * cols * LEV
    lane = lax.broadcasted_iota(jnp.int32, (n_tok, 16), 1)
    level = lax.broadcasted_iota(jnp.int32, (n_tok, 16), 0) % LEV
    lane_level = (lane % LEV == level)
    lane_kind = (lane // LEV).astype(F32)
    for s in range(0, rows, SR):
        spread = jnp.broadcast_to(kinds[s:s + SR][:, None, :], band)
        own = jnp.sum(jnp.where(here, spread, 0.0), axis=-1, keepdims=True).reshape(n_tok, 1)
        hot = jnp.where(lane_level & (lane_kind == own), 1.0, 0.0).astype(BF16)
        e = emb[s:s + SR, :cols].reshape(n_tok, -1).astype(F32) + mm(hot, table_rows)
        emb[s:s + SR, :cols] = e.astype(BF16).reshape(SR, cols, LEV, -1)
        if s == 0:
            pl.semaphore_wait(barrier, len(places))
            first[0].start()
    first[1].start()
    second = shift_up(
        fs, [((0, 3), (0, 6)), ((0, 3), (6, 12)), ((3, 6), (0, 6)), ((0, 3), (12, 24)), ((6, 12), (0, 6))],
        s2, r2,
    )
    back = shift_down(
        fs, fine,
        [((0, 6), (18, 24)), ((9, 12), (0, 12)), ((6, 9), (18, 24)), ((9, 12), (12, 18)), ((9, 12), (18, 24))],
        rows, cols, s3, r3,
    )
    keep = pltpu.make_async_copy(
        part(fs, (0, rows - SR), (0, cols - SC)), part(fine, (SR, rows), (SC, cols)), own_sem.at[0]
    )
    scale = math.log2(math.e) / math.sqrt(HD)
    loaded("wq", "wkv")

    def front(w):
        wr, wc_ = w // 2, w % 2
        e = emb[pl.ds(SR + WR * wr, WR), pl.ds(SC + WC * wc_, WC)].reshape(WIN, -1)
        aft[...] = e
        split_tiles(nat, norm(e))
        yield
        n = jnp.concatenate([by_level(nat, levels, 0, POS) for levels in GROUPS], axis=0)
        q[...] = (mm(n, wq[...]) * scale).astype(BF16)
        yield
        k[...] = mm(n, wkv[:, :512]).astype(BF16)
        yield
        v[...] = mm(n, wkv[:, 512:]).astype(BF16)
        yield
        wrapped = jnp.where((lat == n_lat - 1) & (wr == 1), 2, 0)
        for g, levels in enumerate(GROUPS):
            at = pl.ds(g * GRP, GRP)
            for _ in attention(q.at[at], k.at[at], v.at[at], bias[wrapped + g], att, levels, 0, POS, POS):
                yield
        a = (aft[...].astype(F32) + mm(gather(att, slice(None)), wo[...])).astype(BF16)
        yield
        done[...] = a

    def back_half(w):
        wr, wc_ = w // 2, w % 2
        n = norm(done[...]).astype(BF16)
        yield
        for j in range(0, 2048, 512):
            hid[:, j:j + 512] = gelu(mm(n, w1[:, j:j + 512])).astype(BF16)
            yield
        for j in range(0, 512, 256):
            f = (done[:, j:j + 256].astype(F32) + mm(hid[...], w2[:, j:j + 256])).astype(BF16)
            fs[pl.ds(WR * wr, WR), pl.ds(WC * wc_, WC), :, j:j + 256] = f.reshape(WR, WC, LEV, -1)
            yield

    def window(w, carry):
        for _ in back_half(w - 1):
            pass

        @pl.when(w == 1)
        def _():
            for copy in second[:3]:
                copy.start()
            first[1].wait_recv()

        @pl.when(w == 2)
        def _():
            second[3].start()
            first[0].wait_recv()

        @pl.when(w == 3)
        def _():
            second[4].start()
            back[0].start()
            for copy in first[2:]:
                copy.wait_recv()

        for _ in front(w):
            pass
        return carry

    loaded("bias", "wo")
    for _ in front(0):
        pass
    for copy in first[2:]:
        copy.start()
    loaded("w1", "w2")
    load("wm", "wc", "cbias", "wco")
    lax.fori_loop(1, 4, window, 0)
    back[1].start()
    for _ in back_half(3):
        pass
    for copy in back[2:]:
        copy.start()
    keep.start()

    loaded("wm")
    for copy in second:
        copy.wait_recv()
    f = fs[pl.ds(SR, rows), pl.ds(SC, cols)].reshape(rows // 2, 2, cols // 2, 2, LEV, -1)
    m = norm(jnp.concatenate([f[:, j % 2, :, j // 2].reshape(WIN, -1) for j in range(4)], axis=1)).astype(BF16)
    for j in range(0, 1024, 512):
        cin[:, j:j + 512] = mm(m, wm[:, j:j + 512]).astype(BF16)
    split_tiles(cnat, norm(cin[...]))
    cnat[:, WIN:] = jnp.zeros_like(cnat[:, WIN:])
    nk = jnp.concatenate([by_level(cnat, levels, 0, POS) for levels in GROUPS], axis=0)
    loaded("wc", "cbias", "wco")
    for j in range(0, 1024, 512):
        ck[:, j:j + 512] = mm(nk, wc[:, 1024 + j:1536 + j]).astype(BF16)
        cv[:, j:j + 512] = mm(nk, wc[:, 2048 + j:2560 + j]).astype(BF16)
    wrapped = jnp.where(lat == n_lat - 1, 4, 0)
    third = shift_down(
        cs, coarse, [((3, 6), (0, 6)), ((3, 6), (6, 12)), ((0, 3), (6, 12))], WR, WC, s4, r4
    )
    keep_too = pltpu.make_async_copy(
        part(cs, (0, SR), (0, SC)), part(coarse, (SR, WR), (SC, WC)), own_sem.at[1]
    )
    for half in (1, 0):
        nq = [by_level(cnat, levels, half * POS // 2, QPAD) for levels in GROUPS]
        nq = jnp.concatenate(nq, axis=0)
        for j in range(0, 1024, 512):
            cq[:, j:j + 512] = (mm(nq, wc[:, j:j + 512]) * scale).astype(BF16)
        for g, levels in enumerate(GROUPS):
            at = pl.ds(g * 2 * QPAD, 2 * QPAD)
            keys = pl.ds(g * GRP, GRP)
            for _ in attention(
                cq.at[at], ck.at[keys], cv.at[keys], cbias[wrapped + g * 2 + half],
                catt, levels, half * POS // 2, QPAD, POS // 2,
            ):
                pass
        mixed = gather(catt, slice(half * GRP, (half + 1) * GRP))
        at = slice(half * GRP, (half + 1) * GRP)
        for j in range(0, 1024, 512):
            t = (cin[at, j:j + 512].astype(F32) + mm(mixed, wco[:, j:j + 512])).astype(BF16)
            cs[half * SR:(half + 1) * SR, :, :, j:j + 512] = t.reshape(SR, WC, LEV, -1)
        if half == 1:
            third[0].start()
            third[1].start()
        else:
            third[2].start()
            keep_too.start()
    for copy in back + third:
        copy.wait_recv()
    keep.wait()
    keep_too.wait()
    for copy in first + second + back + third:
        copy.wait_send()


def local(
    n_lat, n_lon, tokens, surface_kind, kind_table, attn_q_w, attn_kv_w, attn_out_w,
    mlp_in_w, mlp_out_w, merge_w, coarse_qkv_w, coarse_out_w,
):
    rows, cols, lev, width = tokens.shape
    consts = [jnp.asarray(a) for a in biases()]
    weights = [attn_q_w, attn_kv_w, attn_out_w, mlp_in_w, mlp_out_w, merge_w, coarse_qkv_w, coarse_out_w]
    hbm = pl.BlockSpec(memory_space=pl.ANY)
    dma = pltpu.SemaphoreType.DMA
    buf = lambda *shape: pltpu.VMEM(shape, BF16)
    frame = buf(rows + SR, cols + SC, lev, width)
    return pl.pallas_call(
        functools.partial(kernel, n_lat, n_lon),
        out_shape=(
            buf(rows, cols, lev, width),
            buf(rows // 2, cols // 2, lev, 2 * width),
        ),
        in_specs=[hbm] * 13,
        out_specs=(hbm, hbm),
        scratch_shapes=[
            *[pltpu.VMEM(a.shape, a.dtype) for a in [surface_kind, kind_table] + consts + weights],
            frame, frame, *[buf(WIN, width)] * 3, *[pltpu.VMEM((width // LANES, WIN, LANES), F32)] * 2,
            buf(WIN, width), buf(WIN, width),
            buf(WIN, 4 * width),
            buf(WIN, 2 * width), buf(4 * QPAD, 2 * width), buf(WIN, 2 * width), buf(WIN, 2 * width),
            pltpu.VMEM((2 * width // LANES, WIN + LEV * (2 * QPAD - POS), LANES), F32),
            pltpu.VMEM((2 * width // LANES, WIN, LANES), F32),
            buf(WR, WC, lev, 2 * width),
            dma((13,)), dma((2,)), dma((5,)), dma((5,)), dma((5,)), dma((5,)), dma((5,)), dma((5,)),
            dma((3,)), dma((3,)),
        ],
        compiler_params=pltpu.CompilerParams(
            collective_id=0, has_side_effects=True, vmem_limit_bytes=60 * 1024 * 1024
        ),
        name="block",
    )(tokens, surface_kind, kind_table, *consts, *weights)


def solution(mesh):
    grid = P("lat", "lon", None, None)
    return jax.shard_map(
        functools.partial(local, mesh.shape["lat"], mesh.shape["lon"]),
        mesh=mesh,
        in_specs=(grid, P("lat", "lon")) + (P(),) * 9,
        out_specs=(grid, grid),
        check_vma=False,
    )
```

```python
import functools
import math

import jax
import jax.numpy as jnp
import numpy as np
from jax import lax
from jax.experimental import pallas as pl
from jax.experimental.pallas import tpu as pltpu
from jax.sharding import PartitionSpec as P

EPS = 1e-05
LEV = 4
WR, WC = 6, 12
SR, SC = WR // 2, WC // 2
WIN = WR * WC * LEV
GRP = WIN // 2
POS = WR * WC
QPAD = 40
GROUPS = ((0, 3), (1, 2))
HD = 64
LANES = 128
F32 = jnp.float32
BF16 = jnp.bfloat16


def biases():
    at = np.arange(GRP)
    level = at // POS

    def masks(half):
        same_level = level[:, None] == level[None, :]
        same_half = half[:, None] == half[None, :]
        ok = [same_level, np.ones_like(same_level), same_level & same_half, same_half]
        return np.where(np.stack(ok), 0.0, -1e30).astype(np.float32)

    full = masks(at % POS // (POS // 2))
    coarse = masks(at % WR // SR)
    halves = np.zeros((4, 2, 2, QPAD, GRP), np.float32)
    halves[:, :, :, :POS // 2] = coarse.reshape(4, 2, 2, POS // 2, GRP).transpose(0, 2, 1, 3, 4)
    return full, halves.reshape(8, 2 * QPAD, GRP)


def norm(v):
    v = v.astype(F32)
    c = v - jnp.mean(v, axis=-1, keepdims=True)
    s = jnp.mean(c * c, axis=-1, keepdims=True)
    return c * lax.rsqrt(s + EPS)


def gelu(x):
    inner = x * (math.sqrt(2 / math.pi) + math.sqrt(2 / math.pi) * 0.044715 * (x * x))
    return 0.5 * x * (1.0 + jnp.tanh(inner))


def mm(a, b):
    return jnp.dot(a, b, preferred_element_type=F32)


def by_level(tokens, levels, start, count):
    rows = [pl.ds(start * LEV + l, count, stride=LEV) for l in levels]
    tiles = [jnp.concatenate([tokens[j, r] for r in rows], axis=0) for j in range(tokens.shape[0])]
    return jnp.concatenate([t.astype(BF16) for t in tiles], axis=1)


def split_tiles(tokens, v):
    for j in range(tokens.shape[0]):
        tokens[j, :v.shape[0]] = v[:, j * LANES:(j + 1) * LANES]


def gather(tokens, rows):
    return jnp.concatenate([tokens[j, rows].astype(BF16) for j in range(tokens.shape[0])], axis=1)


def attention(q, k, v, b, out, levels, start, step, used):
    count, width = q.shape
    low = lax.broadcasted_iota(jnp.int32, (count, 2 * HD), 1) < HD
    zero = jnp.zeros((count, 2 * HD), BF16)
    b = jnp.concatenate([b, b], axis=0)
    for pair in range(width // (2 * HD)):
        lanes = slice(pair * 2 * HD, (pair + 1) * 2 * HD)
        qp = q[:, lanes]
        qq = jnp.concatenate([jnp.where(low, qp, zero), jnp.where(low, zero, qp)], axis=0)
        s = lax.dot_general(
            qq, k[:, lanes], (((1,), (1,)), ((), ())), preferred_element_type=F32
        )
        s = s + b
        p = jnp.exp2(s - jnp.max(s, axis=-1, keepdims=True))
        total = jnp.sum(p, axis=-1, keepdims=True)
        o = mm(p.astype(BF16), v[:, lanes]) / total
        o = jnp.where(low, o[:count], o[count:])
        for i, l in enumerate(levels):
            out[pair, pl.ds(start * LEV + l, used, stride=LEV)] = o[i * step:i * step + used]
        yield


def kernel(
    n_lat, n_lon, x, kind_h, table_h, bias_h, cbias_h,
    wq_h, wkv_h, wo_h, w1_h, w2_h, wm_h, wc_h, wco_h,
    fine, coarse,
    kind, table, bias, cbias, wq, wkv, wo, w1, w2, wm, wc, wco,
    emb, fs, q, k, v, nat, att, aft, done, hid, cin, cq, ck, cv, cnat, catt, cs,
    load_sem, own_sem, s1, r1, s2, r2, s3, r3, s4, r4,
):
    lat, lon = lax.axis_index("lat"), lax.axis_index("lon")
    up, down = lax.rem(lat + n_lat - 1, n_lat), lax.rem(lat + 1, n_lat)
    left, right = lax.rem(lon + n_lon - 1, n_lon), lax.rem(lon + 1, n_lon)
    rows, cols = x.shape[0], x.shape[1]

    places = [(down, lon), (lat, right), (down, right)]
    barrier = pltpu.get_barrier_semaphore()
    for a, o in places:
        pl.semaphore_signal(
            barrier, inc=1, device_id={"lat": a, "lon": o}, device_id_type=pl.DeviceIdType.MESH
        )

    loads = {}
    for at, (name, src, dst) in enumerate([
        ("kind", kind_h, kind), ("table", table_h, table), ("x", x, emb.at[pl.ds(0, rows), pl.ds(0, cols)]),
        ("wq", wq_h, wq), ("wkv", wkv_h, wkv), ("bias", bias_h, bias),
        ("wo", wo_h, wo), ("w1", w1_h, w1), ("w2", w2_h, w2),
        ("wm", wm_h, wm), ("wc", wc_h, wc), ("cbias", cbias_h, cbias), ("wco", wco_h, wco),
    ]):
        loads[name] = pltpu.make_async_copy(src, dst, load_sem.at[at])

    def load(*names):
        for name in names:
            loads[name].start()

    def loaded(*names):
        for name in names:
            loads[name].wait()

    load("kind", "table", "x", "wq", "wkv")
    def send(src, dst, ssem, rsem, a, o):
        return pltpu.make_async_remote_copy(
            src_ref=src, dst_ref=dst, send_sem=ssem, recv_sem=rsem,
            device_id={"lat": a, "lon": o}, device_id_type=pl.DeviceIdType.MESH,
        )

    def part(ref, r, c):
        return ref.at[pl.ds(r[0], r[1] - r[0]), pl.ds(c[0], c[1] - c[0])]

    def shift_up(grid, pieces, ssem, rsem):
        out = []
        for at, (r, c) in enumerate(pieces):
            a, o, rr, cc = lat, lon, r, c
            if r[1] <= SR:
                a, rr = up, (r[0] + rows, r[1] + rows)
            if c[1] <= SC:
                o, cc = left, (c[0] + cols, c[1] + cols)
            out.append(send(part(grid, r, c), part(grid, rr, cc), ssem.at[at], rsem.at[at], a, o))
        return out

    def shift_down(grid, place, pieces, n_rows, n_cols, ssem, rsem):
        out = []
        for at, (r, c) in enumerate(pieces):
            a, o = lat, lon
            rr, cc = (r[0] + SR, r[1] + SR), (c[0] + SC, c[1] + SC)
            if rr[0] >= n_rows:
                a, rr = down, (rr[0] - n_rows, rr[1] - n_rows)
            if cc[0] >= n_cols:
                o, cc = right, (cc[0] - n_cols, cc[1] - n_cols)
            out.append(send(part(grid, r, c), part(place, rr, cc), ssem.at[at], rsem.at[at], a, o))
        return out

    first = shift_up(
        emb, [((0, 3), (6, 18)), ((3, 9), (0, 6)), ((0, 3), (18, 24)), ((0, 3), (0, 6)), ((9, 12), (0, 6))],
        s1, r1,
    )

    loaded("kind", "table", "x")
    load("bias", "wo", "w1", "w2")
    kinds = kind[...].astype(F32)
    table_rows = jnp.concatenate([table[...], jnp.zeros_like(table[:1])], axis=0).reshape(16, -1)
    band = (SR, cols * LEV, cols)
    here = lax.broadcasted_iota(jnp.int32, band, 1) // LEV == lax.broadcasted_iota(jnp.int32, band, 2)
    n_tok = SR * cols * LEV
    lane = lax.broadcasted_iota(jnp.int32, (n_tok, 16), 1)
    level = lax.broadcasted_iota(jnp.int32, (n_tok, 16), 0) % LEV
    lane_level = (lane % LEV == level)
    lane_kind = (lane // LEV).astype(F32)
    for s in range(0, rows, SR):
        spread = jnp.broadcast_to(kinds[s:s + SR][:, None, :], band)
        own = jnp.sum(jnp.where(here, spread, 0.0), axis=-1, keepdims=True).reshape(n_tok, 1)
        hot = jnp.where(lane_level & (lane_kind == own), 1.0, 0.0).astype(BF16)
        e = emb[s:s + SR, :cols].reshape(n_tok, -1).astype(F32) + mm(hot, table_rows)
        emb[s:s + SR, :cols] = e.astype(BF16).reshape(SR, cols, LEV, -1)
        if s == 0:
            pl.semaphore_wait(barrier, len(places))
            first[0].start()
    first[1].start()
    second = shift_up(
        fs, [((0, 3), (0, 6)), ((0, 3), (6, 12)), ((3, 6), (0, 6)), ((0, 3), (12, 24)), ((6, 12), (0, 6))],
        s2, r2,
    )
    back = shift_down(
        fs, fine,
        [((0, 6), (18, 24)), ((9, 12), (0, 12)), ((6, 9), (18, 24)), ((9, 12), (12, 18)), ((9, 12), (18, 24))],
        rows, cols, s3, r3,
    )
    keep = pltpu.make_async_copy(
        part(fs, (0, rows - SR), (0, cols - SC)), part(fine, (SR, rows), (SC, cols)), own_sem.at[0]
    )
    scale = math.log2(math.e) / math.sqrt(HD)
    loaded("wq", "wkv")

    def front(w):
        wr, wc_ = w // 2, w % 2
        e = emb[pl.ds(SR + WR * wr, WR), pl.ds(SC + WC * wc_, WC)].reshape(WIN, -1)
        aft[...] = e
        split_tiles(nat, norm(e))
        yield
        n = jnp.concatenate([by_level(nat, levels, 0, POS) for levels in GROUPS], axis=0)
        q[...] = (mm(n, wq[...]) * scale).astype(BF16)
        yield
        k[...] = mm(n, wkv[:, :512]).astype(BF16)
        yield
        v[...] = mm(n, wkv[:, 512:]).astype(BF16)
        yield
        wrapped = jnp.where((lat == n_lat - 1) & (wr == 1), 2, 0)
        for g, levels in enumerate(GROUPS):
            at = pl.ds(g * GRP, GRP)
            for _ in attention(q.at[at], k.at[at], v.at[at], bias[wrapped + g], att, levels, 0, POS, POS):
                yield
        a = (aft[...].astype(F32) + mm(gather(att, slice(None)), wo[...])).astype(BF16)
        yield
        done[...] = a

    def back_half(w):
        wr, wc_ = w // 2, w % 2
        n = norm(done[...]).astype(BF16)
        yield
        for j in range(0, 2048, 512):
            hid[:, j:j + 512] = gelu(mm(n, w1[:, j:j + 512])).astype(BF16)
            yield
        for j in range(0, 512, 256):
            f = (done[:, j:j + 256].astype(F32) + mm(hid[...], w2[:, j:j + 256])).astype(BF16)
            fs[pl.ds(WR * wr, WR), pl.ds(WC * wc_, WC), :, j:j + 256] = f.reshape(WR, WC, LEV, -1)
            yield

    def window(w, carry):
        for _ in back_half(w - 1):
            pass

        @pl.when(w == 1)
        def _():
            for copy in second[:3]:
                copy.start()
            first[1].wait_recv()

        @pl.when(w == 2)
        def _():
            second[3].start()
            first[0].wait_recv()

        @pl.when(w == 3)
        def _():
            second[4].start()
            back[0].start()
            for copy in first[2:]:
                copy.wait_recv()

        for _ in front(w):
            pass
        return carry

    loaded("bias", "wo")
    for _ in front(0):
        pass
    for copy in first[2:]:
        copy.start()
    loaded("w1", "w2")
    load("wm", "wc", "cbias", "wco")
    lax.fori_loop(1, 4, window, 0)
    back[1].start()
    for _ in back_half(3):
        pass
    for copy in back[2:]:
        copy.start()
    keep.start()

    loaded("wm")
    for copy in second:
        copy.wait_recv()
    f = fs[pl.ds(SR, rows), pl.ds(SC, cols)].reshape(rows // 2, 2, cols // 2, 2, LEV, -1)
    f = [jnp.swapaxes(f[:, j % 2, :, j // 2], 0, 1).reshape(WIN, -1) for j in range(4)]
    m = norm(jnp.concatenate(f, axis=1)).astype(BF16)
    for j in range(0, 1024, 512):
        cin[:, j:j + 512] = mm(m, wm[:, j:j + 512]).astype(BF16)
    split_tiles(cnat, norm(cin[...]))
    cnat[:, WIN:] = jnp.zeros_like(cnat[:, WIN:])
    nk = jnp.concatenate([by_level(cnat, levels, 0, POS) for levels in GROUPS], axis=0)
    loaded("wc", "cbias", "wco")
    for j in range(0, 1024, 512):
        ck[:, j:j + 512] = mm(nk, wc[:, 1024 + j:1536 + j]).astype(BF16)
        cv[:, j:j + 512] = mm(nk, wc[:, 2048 + j:2560 + j]).astype(BF16)
    wrapped = jnp.where(lat == n_lat - 1, 4, 0)
    third = shift_down(
        cs, coarse, [((3, 6), (6, 12)), ((0, 3), (6, 12)), ((3, 6), (0, 6))], WR, WC, s4, r4
    )
    keep_too = pltpu.make_async_copy(
        part(cs, (0, SR), (0, SC)), part(coarse, (SR, WR), (SC, WC)), own_sem.at[1]
    )
    for half in (1, 0):
        nq = [by_level(cnat, levels, half * POS // 2, QPAD) for levels in GROUPS]
        nq = jnp.concatenate(nq, axis=0)
        for j in range(0, 1024, 512):
            cq[:, j:j + 512] = (mm(nq, wc[:, j:j + 512]) * scale).astype(BF16)
        for g, levels in enumerate(GROUPS):
            at = pl.ds(g * 2 * QPAD, 2 * QPAD)
            keys = pl.ds(g * GRP, GRP)
            for _ in attention(
                cq.at[at], ck.at[keys], cv.at[keys], cbias[wrapped + g * 2 + half],
                catt, levels, half * POS // 2, QPAD, POS // 2,
            ):
                pass
        mixed = gather(catt, slice(half * GRP, (half + 1) * GRP))
        at = slice(half * GRP, (half + 1) * GRP)
        for j in range(0, 1024, 512):
            t = (cin[at, j:j + 512].astype(F32) + mm(mixed, wco[:, j:j + 512])).astype(BF16)
            t = jnp.swapaxes(t.reshape(SC, WR, LEV, -1), 0, 1)
            cs[:, half * SC:(half + 1) * SC, :, j:j + 512] = t
        if half == 1:
            third[0].start()
            third[1].start()
        else:
            third[2].start()
            keep_too.start()
    for copy in back + third:
        copy.wait_recv()
    keep.wait()
    keep_too.wait()
    for copy in first + second + back + third:
        copy.wait_send()


def local(
    n_lat, n_lon, tokens, surface_kind, kind_table, attn_q_w, attn_kv_w, attn_out_w,
    mlp_in_w, mlp_out_w, merge_w, coarse_qkv_w, coarse_out_w,
):
    rows, cols, lev, width = tokens.shape
    consts = [jnp.asarray(a) for a in biases()]
    weights = [attn_q_w, attn_kv_w, attn_out_w, mlp_in_w, mlp_out_w, merge_w, coarse_qkv_w, coarse_out_w]
    hbm = pl.BlockSpec(memory_space=pl.ANY)
    dma = pltpu.SemaphoreType.DMA
    buf = lambda *shape: pltpu.VMEM(shape, BF16)
    frame = buf(rows + SR, cols + SC, lev, width)
    return pl.pallas_call(
        functools.partial(kernel, n_lat, n_lon),
        out_shape=(
            buf(rows, cols, lev, width),
            buf(rows // 2, cols // 2, lev, 2 * width),
        ),
        in_specs=[hbm] * 13,
        out_specs=(hbm, hbm),
        scratch_shapes=[
            *[pltpu.VMEM(a.shape, a.dtype) for a in [surface_kind, kind_table] + consts + weights],
            frame, frame, *[buf(WIN, width)] * 3, *[pltpu.VMEM((width // LANES, WIN, LANES), F32)] * 2,
            buf(WIN, width), buf(WIN, width),
            buf(WIN, 4 * width),
            buf(WIN, 2 * width), buf(4 * QPAD, 2 * width), buf(WIN, 2 * width), buf(WIN, 2 * width),
            pltpu.VMEM((2 * width // LANES, WIN + LEV * (2 * QPAD - POS), LANES), F32),
            pltpu.VMEM((2 * width // LANES, WIN, LANES), F32),
            buf(WR, WC, lev, 2 * width),
            dma((13,)), dma((2,)), dma((5,)), dma((5,)), dma((5,)), dma((5,)), dma((5,)), dma((5,)),
            dma((3,)), dma((3,)),
        ],
        compiler_params=pltpu.CompilerParams(
            collective_id=0, has_side_effects=True, vmem_limit_bytes=60 * 1024 * 1024
        ),
        name="block",
    )(tokens, surface_kind, kind_table, *consts, *weights)


def solution(mesh):
    grid = P("lat", "lon", None, None)
    return jax.shard_map(
        functools.partial(local, mesh.shape["lat"], mesh.shape["lon"]),
        mesh=mesh,
        in_specs=(grid, P("lat", "lon")) + (P(),) * 9,
        out_specs=(grid, grid),
        check_vma=False,
    )
```

```python
import functools
import math

import jax
import jax.numpy as jnp
import numpy as np
from jax import lax
from jax.experimental import pallas as pl
from jax.experimental.pallas import tpu as pltpu
from jax.sharding import PartitionSpec as P

EPS = 1e-05
LEV = 4
WR, WC = 6, 12
SR, SC = WR // 2, WC // 2
WIN = WR * WC * LEV
GRP = WIN // 2
POS = WR * WC
QPAD = 40
GROUPS = ((0, 3), (1, 2))
HD = 64
LANES = 128
F32 = jnp.float32
BF16 = jnp.bfloat16


def biases():
    at = np.arange(GRP)
    level = at // POS

    def masks(half):
        same_level = level[:, None] == level[None, :]
        same_half = half[:, None] == half[None, :]
        ok = [same_level, np.ones_like(same_level), same_level & same_half, same_half]
        return np.where(np.stack(ok), 0.0, -1e30).astype(np.float32)

    full = masks(at % POS // (POS // 2))
    coarse = masks(at % WR // SR)
    halves = np.zeros((4, 2, 2, QPAD, GRP), np.float32)
    halves[:, :, :, :POS // 2] = coarse.reshape(4, 2, 2, POS // 2, GRP).transpose(0, 2, 1, 3, 4)
    return full, halves.reshape(8, 2 * QPAD, GRP)


def norm(v):
    v = v.astype(F32)
    c = v - jnp.mean(v, axis=-1, keepdims=True)
    s = jnp.mean(c * c, axis=-1, keepdims=True)
    return c * lax.rsqrt(s + EPS)


def gelu(x):
    inner = x * (math.sqrt(2 / math.pi) + math.sqrt(2 / math.pi) * 0.044715 * (x * x))
    return 0.5 * x * (1.0 + jnp.tanh(inner))


def mm(a, b):
    return jnp.dot(a, b, preferred_element_type=F32)


def by_level(tokens, levels, start, count):
    rows = [pl.ds(start * LEV + l, count, stride=LEV) for l in levels]
    tiles = [jnp.concatenate([tokens[j, r] for r in rows], axis=0) for j in range(tokens.shape[0])]
    return jnp.concatenate([t.astype(BF16) for t in tiles], axis=1)


def split_tiles(tokens, v):
    for j in range(tokens.shape[0]):
        tokens[j, :v.shape[0]] = v[:, j * LANES:(j + 1) * LANES]


def gather(tokens, rows):
    return jnp.concatenate([tokens[j, rows].astype(BF16) for j in range(tokens.shape[0])], axis=1)


def attention(q, k, v, b, out, levels, start, step, used):
    count, width = q.shape
    low = lax.broadcasted_iota(jnp.int32, (count, 2 * HD), 1) < HD
    zero = jnp.zeros((count, 2 * HD), BF16)
    b = jnp.concatenate([b, b], axis=0)
    for pair in range(width // (2 * HD)):
        lanes = slice(pair * 2 * HD, (pair + 1) * 2 * HD)
        qp = q[:, lanes]
        qq = jnp.concatenate([jnp.where(low, qp, zero), jnp.where(low, zero, qp)], axis=0)
        s = lax.dot_general(
            qq, k[:, lanes], (((1,), (1,)), ((), ())), preferred_element_type=F32
        )
        s = s + b
        p = jnp.exp2(s - jnp.max(s, axis=-1, keepdims=True))
        total = jnp.sum(p, axis=-1, keepdims=True)
        o = mm(p.astype(BF16), v[:, lanes]) / total
        o = jnp.where(low, o[:count], o[count:])
        for i, l in enumerate(levels):
            out[pair, pl.ds(start * LEV + l, used, stride=LEV)] = o[i * step:i * step + used]
        yield


def kernel(
    n_lat, n_lon, x, kind_h, table_h, bias_h, cbias_h,
    wq_h, wkv_h, wo_h, w1_h, w2_h, wm_h, wc_h, wco_h,
    fine, coarse,
    kind, table, bias, cbias, wq, wkv, wo, w1, w2, wm, wc, wco,
    emb, fs, q, k, v, nat, att, aft, done, hid, cin, cq, ck, cv, cnat, catt, cs,
    load_sem, own_sem, s1, r1, s2, r2, s3, r3, s4, r4,
):
    lat, lon = lax.axis_index("lat"), lax.axis_index("lon")
    lat_from, lat_to = lax.rem(lat + n_lat - 1, n_lat), lax.rem(lat + 1, n_lat)
    lon_from, lon_to = lax.rem(lon + n_lon - 1, n_lon), lax.rem(lon + 1, n_lon)
    rows, cols = x.shape[0], x.shape[1]

    places = [(lat_from, lon), (lat, lon_from), (lat_from, lon_from)]
    barrier = pltpu.get_barrier_semaphore()
    for a, o in places:
        pl.semaphore_signal(
            barrier, inc=1, device_id={"lat": a, "lon": o}, device_id_type=pl.DeviceIdType.MESH
        )

    loads = {}
    for at, (name, src, dst) in enumerate([
        ("kind", kind_h, kind), ("table", table_h, table), ("x", x, emb.at[pl.ds(SR, rows), pl.ds(SC, cols)]),
        ("wq", wq_h, wq), ("wkv", wkv_h, wkv), ("bias", bias_h, bias),
        ("wo", wo_h, wo), ("w1", w1_h, w1), ("w2", w2_h, w2),
        ("wm", wm_h, wm), ("wc", wc_h, wc), ("cbias", cbias_h, cbias), ("wco", wco_h, wco),
    ]):
        loads[name] = pltpu.make_async_copy(src, dst, load_sem.at[at])

    def load(*names):
        for name in names:
            loads[name].start()

    def loaded(*names):
        for name in names:
            loads[name].wait()

    load("kind", "table", "x", "wq", "wkv")
    def send(src, dst, ssem, rsem, a, o):
        return pltpu.make_async_remote_copy(
            src_ref=src, dst_ref=dst, send_sem=ssem, recv_sem=rsem,
            device_id={"lat": a, "lon": o}, device_id_type=pl.DeviceIdType.MESH,
        )

    def part(ref, r, c):
        r0, c0 = ref.shape[0] - r[1], ref.shape[1] - c[1]
        return ref.at[pl.ds(r0, r[1] - r[0]), pl.ds(c0, c[1] - c[0])]

    def forward(grid, pieces, ssem, rsem):
        out = []
        for at, (r, c) in enumerate(pieces):
            a, o, rr, cc = lat, lon, r, c
            if r[1] <= SR:
                a, rr = lat_to, (r[0] + rows, r[1] + rows)
            if c[1] <= SC:
                o, cc = lon_to, (c[0] + cols, c[1] + cols)
            out.append(send(part(grid, r, c), part(grid, rr, cc), ssem.at[at], rsem.at[at], a, o))
        return out

    def backward(grid, place, pieces, n_rows, n_cols, ssem, rsem):
        out = []
        for at, (r, c) in enumerate(pieces):
            a, o = lat, lon
            rr, cc = (r[0] + SR, r[1] + SR), (c[0] + SC, c[1] + SC)
            if rr[0] >= n_rows:
                a, rr = lat_from, (rr[0] - n_rows, rr[1] - n_rows)
            if cc[0] >= n_cols:
                o, cc = lon_from, (cc[0] - n_cols, cc[1] - n_cols)
            out.append(send(part(grid, r, c), part(place, rr, cc), ssem.at[at], rsem.at[at], a, o))
        return out

    first = forward(
        emb, [((0, 3), (6, 18)), ((3, 9), (0, 6)), ((0, 3), (18, 24)), ((0, 3), (0, 6)), ((9, 12), (0, 6))],
        s1, r1,
    )

    loaded("kind", "table", "x")
    load("bias", "wo", "w1", "w2")
    kinds = kind[...].astype(F32)
    table_rows = jnp.concatenate([table[...], jnp.zeros_like(table[:1])], axis=0).reshape(16, -1)
    band = (SR, cols * LEV, cols)
    here = lax.broadcasted_iota(jnp.int32, band, 1) // LEV == lax.broadcasted_iota(jnp.int32, band, 2)
    n_tok = SR * cols * LEV
    lane = lax.broadcasted_iota(jnp.int32, (n_tok, 16), 1)
    level = lax.broadcasted_iota(jnp.int32, (n_tok, 16), 0) % LEV
    lane_level = (lane % LEV == level)
    lane_kind = (lane // LEV).astype(F32)
    for s in reversed(range(0, rows, SR)):
        spread = jnp.broadcast_to(kinds[s:s + SR][:, None, :], band)
        own = jnp.sum(jnp.where(here, spread, 0.0), axis=-1, keepdims=True).reshape(n_tok, 1)
        hot = jnp.where(lane_level & (lane_kind == own), 1.0, 0.0).astype(BF16)
        e = emb[SR + s:SR + s + SR, SC:].reshape(n_tok, -1).astype(F32) + mm(hot, table_rows)
        emb[SR + s:SR + s + SR, SC:] = e.astype(BF16).reshape(SR, cols, LEV, -1)
        if s == rows - SR:
            pl.semaphore_wait(barrier, len(places))
            first[0].start()
    first[1].start()
    second = forward(
        fs, [((0, 3), (0, 6)), ((0, 3), (6, 12)), ((3, 6), (0, 6)), ((0, 3), (12, 24)), ((6, 12), (0, 6))],
        s2, r2,
    )
    back = backward(
        fs, fine,
        [((0, 6), (18, 24)), ((9, 12), (0, 12)), ((6, 9), (18, 24)), ((9, 12), (12, 18)), ((9, 12), (18, 24))],
        rows, cols, s3, r3,
    )
    keep = pltpu.make_async_copy(
        part(fs, (0, rows - SR), (0, cols - SC)), part(fine, (SR, rows), (SC, cols)), own_sem.at[0]
    )
    scale = math.log2(math.e) / math.sqrt(HD)
    loaded("wq", "wkv")

    def front(w):
        wr, wc_ = 1 - w // 2, 1 - w % 2
        e = emb[pl.ds(WR * wr, WR), pl.ds(WC * wc_, WC)].reshape(WIN, -1)
        aft[...] = e
        split_tiles(nat, norm(e))
        yield
        n = jnp.concatenate([by_level(nat, levels, 0, POS) for levels in GROUPS], axis=0)
        q[...] = (mm(n, wq[...]) * scale).astype(BF16)
        yield
        k[...] = mm(n, wkv[:, :512]).astype(BF16)
        yield
        v[...] = mm(n, wkv[:, 512:]).astype(BF16)
        yield
        wrapped = jnp.where((lat == 0) & (wr == 0), 2, 0)
        for g, levels in enumerate(GROUPS):
            at = pl.ds(g * GRP, GRP)
            for _ in attention(q.at[at], k.at[at], v.at[at], bias[wrapped + g], att, levels, 0, POS, POS):
                yield
        a = (aft[...].astype(F32) + mm(gather(att, slice(None)), wo[...])).astype(BF16)
        yield
        done[...] = a

    def back_half(w):
        wr, wc_ = 1 - w // 2, 1 - w % 2
        n = norm(done[...]).astype(BF16)
        yield
        for j in range(0, 2048, 512):
            hid[:, j:j + 512] = gelu(mm(n, w1[:, j:j + 512])).astype(BF16)
            yield
        for j in range(0, 512, 256):
            f = (done[:, j:j + 256].astype(F32) + mm(hid[...], w2[:, j:j + 256])).astype(BF16)
            fs[pl.ds(SR + WR * wr, WR), pl.ds(SC + WC * wc_, WC), :, j:j + 256] = f.reshape(WR, WC, LEV, -1)
            yield

    def window(w, carry):
        for _ in back_half(w - 1):
            pass

        @pl.when(w == 1)
        def _():
            for copy in second[:3]:
                copy.start()
            first[1].wait_recv()

        @pl.when(w == 2)
        def _():
            second[3].start()
            first[0].wait_recv()

        @pl.when(w == 3)
        def _():
            second[4].start()
            back[0].start()
            for copy in first[2:]:
                copy.wait_recv()

        for _ in front(w):
            pass
        return carry

    loaded("bias", "wo")
    for _ in front(0):
        pass
    for copy in first[2:]:
        copy.start()
    loaded("w1", "w2")
    load("wm", "wc", "cbias", "wco")
    lax.fori_loop(1, 4, window, 0)
    back[1].start()
    for _ in back_half(3):
        pass
    for copy in back[2:]:
        copy.start()
    keep.start()

    loaded("wm")
    for copy in second:
        copy.wait_recv()
    f = fs[pl.ds(0, rows), pl.ds(0, cols)].reshape(rows // 2, 2, cols // 2, 2, LEV, -1)
    f = [jnp.swapaxes(f[:, j % 2, :, j // 2], 0, 1).reshape(WIN, -1) for j in range(4)]
    m = norm(jnp.concatenate(f, axis=1)).astype(BF16)
    for j in range(0, 1024, 512):
        cin[:, j:j + 512] = mm(m, wm[:, j:j + 512]).astype(BF16)
    split_tiles(cnat, norm(cin[...]))
    cnat[:, WIN:] = jnp.zeros_like(cnat[:, WIN:])
    nk = jnp.concatenate([by_level(cnat, levels, 0, POS) for levels in GROUPS], axis=0)
    loaded("wc", "cbias", "wco")
    for j in range(0, 1024, 512):
        ck[:, j:j + 512] = mm(nk, wc[:, 1024 + j:1536 + j]).astype(BF16)
        cv[:, j:j + 512] = mm(nk, wc[:, 2048 + j:2560 + j]).astype(BF16)
    wrapped = jnp.where(lat == 0, 4, 0)
    third = backward(
        cs, coarse, [((3, 6), (6, 12)), ((0, 3), (6, 12)), ((3, 6), (0, 6))], WR, WC, s4, r4
    )
    keep_too = pltpu.make_async_copy(
        part(cs, (0, SR), (0, SC)), part(coarse, (SR, WR), (SC, WC)), own_sem.at[1]
    )
    for half in (0, 1):
        nq = [by_level(cnat, levels, half * POS // 2, QPAD) for levels in GROUPS]
        nq = jnp.concatenate(nq, axis=0)
        for j in range(0, 1024, 512):
            cq[:, j:j + 512] = (mm(nq, wc[:, j:j + 512]) * scale).astype(BF16)
        for g, levels in enumerate(GROUPS):
            at = pl.ds(g * 2 * QPAD, 2 * QPAD)
            keys = pl.ds(g * GRP, GRP)
            for _ in attention(
                cq.at[at], ck.at[keys], cv.at[keys], cbias[wrapped + g * 2 + half],
                catt, levels, half * POS // 2, QPAD, POS // 2,
            ):
                pass
        mixed = gather(catt, slice(half * GRP, (half + 1) * GRP))
        at = slice(half * GRP, (half + 1) * GRP)
        for j in range(0, 1024, 512):
            t = (cin[at, j:j + 512].astype(F32) + mm(mixed, wco[:, j:j + 512])).astype(BF16)
            t = jnp.swapaxes(t.reshape(SC, WR, LEV, -1), 0, 1)
            cs[:, half * SC:(half + 1) * SC, :, j:j + 512] = t
        if half == 0:
            third[0].start()
            third[1].start()
        else:
            third[2].start()
            keep_too.start()
    for copy in back + third:
        copy.wait_recv()
    keep.wait()
    keep_too.wait()
    for copy in first + second + back + third:
        copy.wait_send()


def local(
    n_lat, n_lon, tokens, surface_kind, kind_table, attn_q_w, attn_kv_w, attn_out_w,
    mlp_in_w, mlp_out_w, merge_w, coarse_qkv_w, coarse_out_w,
):
    rows, cols, lev, width = tokens.shape
    consts = [jnp.asarray(a) for a in biases()]
    weights = [attn_q_w, attn_kv_w, attn_out_w, mlp_in_w, mlp_out_w, merge_w, coarse_qkv_w, coarse_out_w]
    hbm = pl.BlockSpec(memory_space=pl.ANY)
    dma = pltpu.SemaphoreType.DMA
    buf = lambda *shape: pltpu.VMEM(shape, BF16)
    frame = buf(rows + SR, cols + SC, lev, width)
    return pl.pallas_call(
        functools.partial(kernel, n_lat, n_lon),
        out_shape=(
            buf(rows, cols, lev, width),
            buf(rows // 2, cols // 2, lev, 2 * width),
        ),
        in_specs=[hbm] * 13,
        out_specs=(hbm, hbm),
        scratch_shapes=[
            *[pltpu.VMEM(a.shape, a.dtype) for a in [surface_kind, kind_table] + consts + weights],
            frame, frame, *[buf(WIN, width)] * 3, *[pltpu.VMEM((width // LANES, WIN, LANES), F32)] * 2,
            buf(WIN, width), buf(WIN, width),
            buf(WIN, 4 * width),
            buf(WIN, 2 * width), buf(4 * QPAD, 2 * width), buf(WIN, 2 * width), buf(WIN, 2 * width),
            pltpu.VMEM((2 * width // LANES, WIN + LEV * (2 * QPAD - POS), LANES), F32),
            pltpu.VMEM((2 * width // LANES, WIN, LANES), F32),
            buf(WR, WC, lev, 2 * width),
            dma((13,)), dma((2,)), dma((5,)), dma((5,)), dma((5,)), dma((5,)), dma((5,)), dma((5,)),
            dma((3,)), dma((3,)),
        ],
        compiler_params=pltpu.CompilerParams(
            collective_id=0, has_side_effects=True, vmem_limit_bytes=60 * 1024 * 1024
        ),
        name="block",
    )(tokens, surface_kind, kind_table, *consts, *weights)


def solution(mesh):
    grid = P("lat", "lon", None, None)
    return jax.shard_map(
        functools.partial(local, mesh.shape["lat"], mesh.shape["lon"]),
        mesh=mesh,
        in_specs=(grid, P("lat", "lon")) + (P(),) * 9,
        out_specs=(grid, grid),
        check_vma=False,
    )
```

```python
import functools
import math

import jax
import jax.numpy as jnp
import numpy as np
from jax import lax
from jax.experimental import pallas as pl
from jax.experimental.pallas import tpu as pltpu
from jax.sharding import PartitionSpec as P

EPS = 1e-05
LEV = 4
WR, WC = 6, 12
SR, SC = WR // 2, WC // 2
WIN = WR * WC * LEV
GRP = WIN // 2
POS = WR * WC
QPAD = 40
GROUPS = ((0, 3), (1, 2))
HD = 64
LANES = 128
F32 = jnp.float32
BF16 = jnp.bfloat16


def biases():
    at = np.arange(GRP)
    level = at // POS

    def masks(half):
        same_level = level[:, None] == level[None, :]
        same_half = half[:, None] == half[None, :]
        ok = [same_level, np.ones_like(same_level), same_level & same_half, same_half]
        return np.where(np.stack(ok), 0.0, -1e30).astype(np.float32)

    full = masks(at % POS // (POS // 2))
    coarse = full
    halves = np.zeros((4, 2, 2, QPAD, GRP), np.float32)
    halves[:, :, :, :POS // 2] = coarse.reshape(4, 2, 2, POS // 2, GRP).transpose(0, 2, 1, 3, 4)
    return full, halves.reshape(8, 2 * QPAD, GRP)


def norm(v):
    v = v.astype(F32)
    c = v - jnp.mean(v, axis=-1, keepdims=True)
    s = jnp.mean(c * c, axis=-1, keepdims=True)
    return c * lax.rsqrt(s + EPS)


def gelu(x):
    inner = x * (math.sqrt(2 / math.pi) + math.sqrt(2 / math.pi) * 0.044715 * (x * x))
    return 0.5 * x * (1.0 + jnp.tanh(inner))


def mm(a, b):
    return jnp.dot(a, b, preferred_element_type=F32)


def by_level(tokens, levels, start, count):
    rows = [pl.ds(start * LEV + l, count, stride=LEV) for l in levels]
    tiles = [jnp.concatenate([tokens[j, r] for r in rows], axis=0) for j in range(tokens.shape[0])]
    return jnp.concatenate([t.astype(BF16) for t in tiles], axis=1)


def split_tiles(tokens, v):
    for j in range(tokens.shape[0]):
        tokens[j, :v.shape[0]] = v[:, j * LANES:(j + 1) * LANES]


def gather(tokens, rows):
    return jnp.concatenate([tokens[j, rows].astype(BF16) for j in range(tokens.shape[0])], axis=1)


def attention(q, k, v, b, out, levels, start, step, used):
    count, width = q.shape
    low = lax.broadcasted_iota(jnp.int32, (count, 2 * HD), 1) < HD
    zero = jnp.zeros((count, 2 * HD), BF16)
    b = jnp.concatenate([b, b], axis=0)
    for pair in range(width // (2 * HD)):
        lanes = slice(pair * 2 * HD, (pair + 1) * 2 * HD)
        qp = q[:, lanes]
        qq = jnp.concatenate([jnp.where(low, qp, zero), jnp.where(low, zero, qp)], axis=0)
        s = lax.dot_general(
            qq, k[:, lanes], (((1,), (1,)), ((), ())), preferred_element_type=F32
        )
        s = s + b
        p = jnp.exp2(s - jnp.max(s, axis=-1, keepdims=True))
        total = jnp.sum(p, axis=-1, keepdims=True)
        o = mm(p.astype(BF16), v[:, lanes]) / total
        o = jnp.where(low, o[:count], o[count:])
        for i, l in enumerate(levels):
            out[pair, pl.ds(start * LEV + l, used, stride=LEV)] = o[i * step:i * step + used]
        yield


def kernel(
    n_lat, n_lon, x, kind_h, table_h, bias_h, cbias_h,
    wq_h, wkv_h, wo_h, w1_h, w2_h, wm_h, wc_h, wco_h,
    fine, coarse,
    kind, table, bias, cbias, wq, wkv, wo, w1, w2, wm, wc, wco,
    emb, fs, q, k, v, nat, att, aft, done, hid, cin, cq, ck, cv, cnat, catt, cs,
    load_sem, own_sem, s1, r1, s2, r2, s3, r3, s4, r4,
):
    lat, lon = lax.axis_index("lat"), lax.axis_index("lon")
    lat_from, lat_to = lax.rem(lat + n_lat - 1, n_lat), lax.rem(lat + 1, n_lat)
    lon_from, lon_to = lax.rem(lon + n_lon - 1, n_lon), lax.rem(lon + 1, n_lon)
    rows, cols = x.shape[0], x.shape[1]

    places = [(lat_from, lon), (lat, lon_from), (lat_from, lon_from)]
    barrier = pltpu.get_barrier_semaphore()
    for a, o in places:
        pl.semaphore_signal(
            barrier, inc=1, device_id={"lat": a, "lon": o}, device_id_type=pl.DeviceIdType.MESH
        )

    loads = {}
    for at, (name, src, dst) in enumerate([
        ("kind", kind_h, kind), ("table", table_h, table), ("x", x, emb.at[pl.ds(SR, rows), pl.ds(SC, cols)]),
        ("wq", wq_h, wq), ("wkv", wkv_h, wkv), ("bias", bias_h, bias),
        ("wo", wo_h, wo), ("w1", w1_h, w1), ("w2", w2_h, w2),
        ("wm", wm_h, wm), ("wc", wc_h, wc), ("cbias", cbias_h, cbias), ("wco", wco_h, wco),
    ]):
        loads[name] = pltpu.make_async_copy(src, dst, load_sem.at[at])

    def load(*names):
        for name in names:
            loads[name].start()

    def loaded(*names):
        for name in names:
            loads[name].wait()

    load("kind", "table", "x", "wq", "wkv")
    def send(src, dst, ssem, rsem, a, o):
        return pltpu.make_async_remote_copy(
            src_ref=src, dst_ref=dst, send_sem=ssem, recv_sem=rsem,
            device_id={"lat": a, "lon": o}, device_id_type=pl.DeviceIdType.MESH,
        )

    def part(ref, r, c):
        r0, c0 = ref.shape[0] - r[1], ref.shape[1] - c[1]
        return ref.at[pl.ds(r0, r[1] - r[0]), pl.ds(c0, c[1] - c[0])]

    def forward(grid, pieces, ssem, rsem):
        out = []
        for at, (r, c) in enumerate(pieces):
            a, o, rr, cc = lat, lon, r, c
            if r[1] <= SR:
                a, rr = lat_to, (r[0] + rows, r[1] + rows)
            if c[1] <= SC:
                o, cc = lon_to, (c[0] + cols, c[1] + cols)
            out.append(send(part(grid, r, c), part(grid, rr, cc), ssem.at[at], rsem.at[at], a, o))
        return out

    def backward(grid, place, pieces, n_rows, n_cols, ssem, rsem):
        out = []
        for at, (r, c) in enumerate(pieces):
            a, o = lat, lon
            rr, cc = (r[0] + SR, r[1] + SR), (c[0] + SC, c[1] + SC)
            if rr[0] >= n_rows:
                a, rr = lat_from, (rr[0] - n_rows, rr[1] - n_rows)
            if cc[0] >= n_cols:
                o, cc = lon_from, (cc[0] - n_cols, cc[1] - n_cols)
            out.append(send(part(grid, r, c), part(place, rr, cc), ssem.at[at], rsem.at[at], a, o))
        return out

    first = forward(
        emb, [((0, 3), (6, 18)), ((3, 9), (0, 6)), ((0, 3), (18, 24)), ((0, 3), (0, 6)), ((9, 12), (0, 6))],
        s1, r1,
    )

    loaded("kind", "table", "x")
    load("bias", "wo", "w1", "w2")
    kinds = kind[...].astype(F32)
    table_rows = jnp.concatenate([table[...], jnp.zeros_like(table[:1])], axis=0).reshape(16, -1)
    band = (SR, cols * LEV, cols)
    here = lax.broadcasted_iota(jnp.int32, band, 1) // LEV == lax.broadcasted_iota(jnp.int32, band, 2)
    n_tok = SR * cols * LEV
    lane = lax.broadcasted_iota(jnp.int32, (n_tok, 16), 1)
    level = lax.broadcasted_iota(jnp.int32, (n_tok, 16), 0) % LEV
    lane_level = (lane % LEV == level)
    lane_kind = (lane // LEV).astype(F32)
    for s in reversed(range(0, rows, SR)):
        spread = jnp.broadcast_to(kinds[s:s + SR][:, None, :], band)
        own = jnp.sum(jnp.where(here, spread, 0.0), axis=-1, keepdims=True).reshape(n_tok, 1)
        hot = jnp.where(lane_level & (lane_kind == own), 1.0, 0.0).astype(BF16)
        e = emb[SR + s:SR + s + SR, SC:].reshape(n_tok, -1).astype(F32) + mm(hot, table_rows)
        emb[SR + s:SR + s + SR, SC:] = e.astype(BF16).reshape(SR, cols, LEV, -1)
        if s == rows - SR:
            pl.semaphore_wait(barrier, len(places))
            first[0].start()
    first[1].start()
    second = forward(
        fs, [((0, 3), (0, 6)), ((0, 3), (6, 12)), ((3, 6), (0, 6)), ((0, 3), (12, 24)), ((6, 12), (0, 6))],
        s2, r2,
    )
    back = backward(
        fs, fine,
        [((0, 6), (18, 24)), ((9, 12), (0, 12)), ((6, 9), (18, 24)), ((9, 12), (12, 18)), ((9, 12), (18, 24))],
        rows, cols, s3, r3,
    )
    keep = pltpu.make_async_copy(
        part(fs, (0, rows - SR), (0, cols - SC)), part(fine, (SR, rows), (SC, cols)), own_sem.at[0]
    )
    scale = math.log2(math.e) / math.sqrt(HD)
    loaded("wq", "wkv")

    def front(w):
        wr, wc_ = 1 - w // 2, 1 - w % 2
        e = emb[pl.ds(WR * wr, WR), pl.ds(WC * wc_, WC)].reshape(WIN, -1)
        aft[...] = e
        split_tiles(nat, norm(e))
        yield
        n = jnp.concatenate([by_level(nat, levels, 0, POS) for levels in GROUPS], axis=0)
        q[...] = (mm(n, wq[...]) * scale).astype(BF16)
        yield
        k[...] = mm(n, wkv[:, :512]).astype(BF16)
        yield
        v[...] = mm(n, wkv[:, 512:]).astype(BF16)
        yield
        wrapped = jnp.where((lat == 0) & (wr == 0), 2, 0)
        for g, levels in enumerate(GROUPS):
            at = pl.ds(g * GRP, GRP)
            for _ in attention(q.at[at], k.at[at], v.at[at], bias[wrapped + g], att, levels, 0, POS, POS):
                yield
        a = (aft[...].astype(F32) + mm(gather(att, slice(None)), wo[...])).astype(BF16)
        yield
        done[...] = a

    def back_half(w):
        wr, wc_ = 1 - w // 2, 1 - w % 2
        n = norm(done[...]).astype(BF16)
        yield
        for j in range(0, 2048, 512):
            hid[:, j:j + 512] = gelu(mm(n, w1[:, j:j + 512])).astype(BF16)
            yield
        for j in range(0, 512, 256):
            f = (done[:, j:j + 256].astype(F32) + mm(hid[...], w2[:, j:j + 256])).astype(BF16)
            fs[pl.ds(SR + WR * wr, WR), pl.ds(SC + WC * wc_, WC), :, j:j + 256] = f.reshape(WR, WC, LEV, -1)
            yield

    def window(w, carry):
        for _ in back_half(w - 1):
            pass

        @pl.when(w == 1)
        def _():
            for copy in first[2:4] + second[:3]:
                copy.start()
            first[1].wait_recv()

        @pl.when(w == 2)
        def _():
            second[3].start()
            back[0].start()
            first[0].wait_recv()

        @pl.when(w == 3)
        def _():
            second[4].start()
            back[1].start()
            for copy in first[2:]:
                copy.wait_recv()

        for _ in front(w):
            pass
        return carry

    loaded("bias", "wo")
    for _ in front(0):
        pass
    first[4].start()
    loaded("w1", "w2")
    load("wm", "wc", "cbias", "wco")
    lax.fori_loop(1, 4, window, 0)
    for _ in back_half(3):
        pass
    for copy in back[2:]:
        copy.start()
    keep.start()

    loaded("wm")
    for copy in second:
        copy.wait_recv()
    f = fs[pl.ds(0, rows), pl.ds(0, cols)].reshape(rows // 2, 2, cols // 2, 2, LEV, -1)
    f = [f[:, j % 2, :, j // 2].reshape(WIN, -1) for j in range(4)]
    m = norm(jnp.concatenate(f, axis=1)).astype(BF16)
    for j in range(0, 1024, 512):
        cin[:, j:j + 512] = mm(m, wm[:, j:j + 512]).astype(BF16)
    split_tiles(cnat, norm(cin[...]))
    cnat[:, WIN:] = jnp.zeros_like(cnat[:, WIN:])
    nk = jnp.concatenate([by_level(cnat, levels, 0, POS) for levels in GROUPS], axis=0)
    loaded("wc", "cbias", "wco")
    for j in range(0, 1024, 512):
        ck[:, j:j + 512] = mm(nk, wc[:, 1024 + j:1536 + j]).astype(BF16)
        cv[:, j:j + 512] = mm(nk, wc[:, 2048 + j:2560 + j]).astype(BF16)
    wrapped = jnp.where(lat == 0, 4, 0)
    third = backward(
        cs, coarse, [((3, 6), (6, 12)), ((3, 6), (0, 6)), ((0, 3), (6, 12))], WR, WC, s4, r4
    )
    keep_too = pltpu.make_async_copy(
        part(cs, (0, SR), (0, SC)), part(coarse, (SR, WR), (SC, WC)), own_sem.at[1]
    )
    for half in (0, 1):
        nq = [by_level(cnat, levels, half * POS // 2, QPAD) for levels in GROUPS]
        nq = jnp.concatenate(nq, axis=0)
        for j in range(0, 1024, 512):
            cq[:, j:j + 512] = (mm(nq, wc[:, j:j + 512]) * scale).astype(BF16)
        for g, levels in enumerate(GROUPS):
            at = pl.ds(g * 2 * QPAD, 2 * QPAD)
            keys = pl.ds(g * GRP, GRP)
            for _ in attention(
                cq.at[at], ck.at[keys], cv.at[keys], cbias[wrapped + g * 2 + half],
                catt, levels, half * POS // 2, QPAD, POS // 2,
            ):
                pass
        mixed = gather(catt, slice(half * GRP, (half + 1) * GRP))
        at = slice(half * GRP, (half + 1) * GRP)
        for j in range(0, 1024, 512):
            t = (cin[at, j:j + 512].astype(F32) + mm(mixed, wco[:, j:j + 512])).astype(BF16)
            cs[half * SR:(half + 1) * SR, :, :, j:j + 512] = t.reshape(SR, WC, LEV, -1)
        if half == 0:
            third[0].start()
            third[1].start()
        else:
            third[2].start()
            keep_too.start()
    for copy in back + third:
        copy.wait_recv()
    keep.wait()
    keep_too.wait()
    for copy in first + second + back + third:
        copy.wait_send()


def local(
    n_lat, n_lon, tokens, surface_kind, kind_table, attn_q_w, attn_kv_w, attn_out_w,
    mlp_in_w, mlp_out_w, merge_w, coarse_qkv_w, coarse_out_w,
):
    rows, cols, lev, width = tokens.shape
    consts = [jnp.asarray(a) for a in biases()]
    weights = [attn_q_w, attn_kv_w, attn_out_w, mlp_in_w, mlp_out_w, merge_w, coarse_qkv_w, coarse_out_w]
    hbm = pl.BlockSpec(memory_space=pl.ANY)
    dma = pltpu.SemaphoreType.DMA
    buf = lambda *shape: pltpu.VMEM(shape, BF16)
    frame = buf(rows + SR, cols + SC, lev, width)
    return pl.pallas_call(
        functools.partial(kernel, n_lat, n_lon),
        out_shape=(
            buf(rows, cols, lev, width),
            buf(rows // 2, cols // 2, lev, 2 * width),
        ),
        in_specs=[hbm] * 13,
        out_specs=(hbm, hbm),
        scratch_shapes=[
            *[pltpu.VMEM(a.shape, a.dtype) for a in [surface_kind, kind_table] + consts + weights],
            frame, frame, *[buf(WIN, width)] * 3, *[pltpu.VMEM((width // LANES, WIN, LANES), F32)] * 2,
            buf(WIN, width), buf(WIN, width),
            buf(WIN, 4 * width),
            buf(WIN, 2 * width), buf(4 * QPAD, 2 * width), buf(WIN, 2 * width), buf(WIN, 2 * width),
            pltpu.VMEM((2 * width // LANES, WIN + LEV * (2 * QPAD - POS), LANES), F32),
            pltpu.VMEM((2 * width // LANES, WIN, LANES), F32),
            buf(WR, WC, lev, 2 * width),
            dma((13,)), dma((2,)), dma((5,)), dma((5,)), dma((5,)), dma((5,)), dma((5,)), dma((5,)),
            dma((3,)), dma((3,)),
        ],
        compiler_params=pltpu.CompilerParams(
            collective_id=0, has_side_effects=True, vmem_limit_bytes=60 * 1024 * 1024
        ),
        name="block",
    )(tokens, surface_kind, kind_table, *consts, *weights)


def solution(mesh):
    grid = P("lat", "lon", None, None)
    return jax.shard_map(
        functools.partial(local, mesh.shape["lat"], mesh.shape["lon"]),
        mesh=mesh,
        in_specs=(grid, P("lat", "lon")) + (P(),) * 9,
        out_specs=(grid, grid),
        check_vma=False,
    )
```

```python
import functools
import math

import jax
import jax.numpy as jnp
import numpy as np
from jax import lax
from jax.experimental import pallas as pl
from jax.experimental.pallas import tpu as pltpu
from jax.sharding import PartitionSpec as P

EPS = 1e-05
LEV = 4
WR, WC = 6, 12
SR, SC = WR // 2, WC // 2
WIN = WR * WC * LEV
GRP = WIN // 2
POS = WR * WC
QPAD = 40
GROUPS = ((0, 3), (1, 2))
HD = 64
LANES = 128
F32 = jnp.float32
BF16 = jnp.bfloat16


def biases():
    at = np.arange(GRP)
    level = at // POS

    def masks(half):
        same_level = level[:, None] == level[None, :]
        same_half = half[:, None] == half[None, :]
        ok = [same_level, np.ones_like(same_level), same_level & same_half, same_half]
        return np.where(np.stack(ok), 0.0, -1e30).astype(np.float32)

    full = masks(at % POS // (POS // 2))
    coarse = full
    halves = np.zeros((4, 2, 2, QPAD, GRP), np.float32)
    halves[:, :, :, :POS // 2] = coarse.reshape(4, 2, 2, POS // 2, GRP).transpose(0, 2, 1, 3, 4)
    return full, halves.reshape(8, 2 * QPAD, GRP)


def norm(v):
    v = v.astype(F32)
    c = v - jnp.mean(v, axis=-1, keepdims=True)
    s = jnp.mean(c * c, axis=-1, keepdims=True)
    return c * lax.rsqrt(s + EPS)


def gelu(x):
    inner = x * (math.sqrt(2 / math.pi) + math.sqrt(2 / math.pi) * 0.044715 * (x * x))
    return 0.5 * x * (1.0 + jnp.tanh(inner))


def mm(a, b):
    return jnp.dot(a, b, preferred_element_type=F32)


def by_level(tokens, levels, start, count):
    rows = [pl.ds(start * LEV + l, count, stride=LEV) for l in levels]
    tiles = [jnp.concatenate([tokens[j, r] for r in rows], axis=0) for j in range(tokens.shape[0])]
    return jnp.concatenate([t.astype(BF16) for t in tiles], axis=1)


def split_tiles(tokens, v):
    for j in range(tokens.shape[0]):
        tokens[j, :v.shape[0]] = v[:, j * LANES:(j + 1) * LANES]


def gather(tokens, rows):
    return jnp.concatenate([tokens[j, rows].astype(BF16) for j in range(tokens.shape[0])], axis=1)


def attention(q, k, v, b, out, levels, start, step, used):
    count, width = q.shape
    low = lax.broadcasted_iota(jnp.int32, (count, 2 * HD), 1) < HD
    zero = jnp.zeros((count, 2 * HD), BF16)
    b = jnp.concatenate([b, b], axis=0)
    for pair in range(width // (2 * HD)):
        lanes = slice(pair * 2 * HD, (pair + 1) * 2 * HD)
        qp = q[:, lanes]
        qq = jnp.concatenate([jnp.where(low, qp, zero), jnp.where(low, zero, qp)], axis=0)
        s = lax.dot_general(
            qq, k[:, lanes], (((1,), (1,)), ((), ())), preferred_element_type=F32
        )
        s = s + b
        p = jnp.exp2(s - jnp.max(s, axis=-1, keepdims=True))
        total = jnp.sum(p, axis=-1, keepdims=True)
        o = mm(p.astype(BF16), v[:, lanes]) / total
        o = jnp.where(low, o[:count], o[count:])
        for i, l in enumerate(levels):
            out[pair, pl.ds(start * LEV + l, used, stride=LEV)] = o[i * step:i * step + used]
        yield


def kernel(
    n_lat, n_lon, x, kind_h, table_h, bias_h, cbias_h,
    wq_h, wkv_h, wo_h, w1_h, w2_h, wm_h, wc_h, wco_h,
    fine, coarse,
    kind, table, bias, cbias, wq, wkv, wo, w1, w2, wm, wc, wco,
    emb, fs, q, k, v, nat, att, aft, done, hid, cin, cq, ck, cv, cnat, catt, cs,
    load_sem, own_sem, s1, r1, s2, r2, s3, r3, s4, r4,
):
    lat, lon = lax.axis_index("lat"), lax.axis_index("lon")
    lat_from, lat_to = lax.rem(lat + n_lat - 1, n_lat), lax.rem(lat + 1, n_lat)
    lon_from, lon_to = lax.rem(lon + n_lon - 1, n_lon), lax.rem(lon + 1, n_lon)
    rows, cols = x.shape[0], x.shape[1]

    places = [(lat_from, lon), (lat, lon_from), (lat_from, lon_from)]
    barrier = pltpu.get_barrier_semaphore()
    for a, o in places:
        pl.semaphore_signal(
            barrier, inc=1, device_id={"lat": a, "lon": o}, device_id_type=pl.DeviceIdType.MESH
        )

    loads = {}
    for at, (name, src, dst) in enumerate([
        ("kind", kind_h, kind), ("table", table_h, table), ("x", x, emb.at[pl.ds(SR, rows), pl.ds(SC, cols)]),
        ("wq", wq_h, wq), ("wkv", wkv_h, wkv), ("bias", bias_h, bias),
        ("wo", wo_h, wo), ("w1", w1_h, w1), ("w2", w2_h, w2),
        ("wm", wm_h, wm), ("wc", wc_h, wc), ("cbias", cbias_h, cbias), ("wco", wco_h, wco),
    ]):
        loads[name] = pltpu.make_async_copy(src, dst, load_sem.at[at])

    def load(*names):
        for name in names:
            loads[name].start()

    def loaded(*names):
        for name in names:
            loads[name].wait()

    load("kind", "table", "x", "wq", "wkv")
    def send(src, dst, ssem, rsem, a, o):
        return pltpu.make_async_remote_copy(
            src_ref=src, dst_ref=dst, send_sem=ssem, recv_sem=rsem,
            device_id={"lat": a, "lon": o}, device_id_type=pl.DeviceIdType.MESH,
        )

    def part(ref, r, c):
        r0, c0 = ref.shape[0] - r[1], ref.shape[1] - c[1]
        return ref.at[pl.ds(r0, r[1] - r[0]), pl.ds(c0, c[1] - c[0])]

    def forward(grid, pieces, ssem, rsem):
        out = []
        for at, (r, c) in enumerate(pieces):
            a, o, rr, cc = lat, lon, r, c
            if r[1] <= SR:
                a, rr = lat_to, (r[0] + rows, r[1] + rows)
            if c[1] <= SC:
                o, cc = lon_to, (c[0] + cols, c[1] + cols)
            out.append(send(part(grid, r, c), part(grid, rr, cc), ssem.at[at], rsem.at[at], a, o))
        return out

    def backward(grid, place, pieces, n_rows, n_cols, ssem, rsem):
        out = []
        for at, (r, c) in enumerate(pieces):
            a, o = lat, lon
            rr, cc = (r[0] + SR, r[1] + SR), (c[0] + SC, c[1] + SC)
            if rr[0] >= n_rows:
                a, rr = lat_from, (rr[0] - n_rows, rr[1] - n_rows)
            if cc[0] >= n_cols:
                o, cc = lon_from, (cc[0] - n_cols, cc[1] - n_cols)
            out.append(send(part(grid, r, c), part(place, rr, cc), ssem.at[at], rsem.at[at], a, o))
        return out

    first = forward(
        emb, [((0, 3), (6, 18)), ((3, 9), (0, 6)), ((0, 3), (18, 24)), ((0, 3), (0, 6)), ((9, 12), (0, 6))],
        s1, r1,
    )

    loaded("kind", "table", "x")
    load("bias", "wo", "w1", "w2")
    kinds = kind[...].astype(F32)
    table_rows = jnp.concatenate([table[...], jnp.zeros_like(table[:1])], axis=0).reshape(16, -1)
    band = (SR, cols * LEV, cols)
    here = lax.broadcasted_iota(jnp.int32, band, 1) // LEV == lax.broadcasted_iota(jnp.int32, band, 2)
    n_tok = SR * cols * LEV
    lane = lax.broadcasted_iota(jnp.int32, (n_tok, 16), 1)
    level = lax.broadcasted_iota(jnp.int32, (n_tok, 16), 0) % LEV
    lane_level = (lane % LEV == level)
    lane_kind = (lane // LEV).astype(F32)
    for s in reversed(range(0, rows, SR)):
        spread = jnp.broadcast_to(kinds[s:s + SR][:, None, :], band)
        own = jnp.sum(jnp.where(here, spread, 0.0), axis=-1, keepdims=True).reshape(n_tok, 1)
        hot = jnp.where(lane_level & (lane_kind == own), 1.0, 0.0).astype(BF16)
        e = emb[SR + s:SR + s + SR, SC:].reshape(n_tok, -1).astype(F32) + mm(hot, table_rows)
        emb[SR + s:SR + s + SR, SC:] = e.astype(BF16).reshape(SR, cols, LEV, -1)
        if s == rows - SR:
            pl.semaphore_wait(barrier, len(places))
            first[0].start()
    first[1].start()
    second = forward(
        fs, [((0, 3), (0, 6)), ((0, 3), (6, 12)), ((3, 6), (0, 6)), ((0, 3), (12, 24)), ((6, 12), (0, 6))],
        s2, r2,
    )
    back = backward(
        fs, fine,
        [((0, 6), (18, 24)), ((9, 12), (0, 12)), ((6, 9), (18, 24)), ((9, 12), (12, 18)), ((9, 12), (18, 24))],
        rows, cols, s3, r3,
    )
    keep = pltpu.make_async_copy(
        part(fs, (0, rows - SR), (0, cols - SC)), part(fine, (SR, rows), (SC, cols)), own_sem.at[0]
    )
    scale = math.log2(math.e) / math.sqrt(HD)
    loaded("wq", "wkv")

    def front(w):
        wr, wc_ = 1 - w // 2, 1 - w % 2
        e = emb[pl.ds(WR * wr, WR), pl.ds(WC * wc_, WC)].reshape(WIN, -1)
        aft[...] = e
        split_tiles(nat, norm(e))
        yield
        n = jnp.concatenate([by_level(nat, levels, 0, POS) for levels in GROUPS], axis=0)
        q[...] = (mm(n, wq[...]) * scale).astype(BF16)
        yield
        k[...] = mm(n, wkv[:, :512]).astype(BF16)
        yield
        v[...] = mm(n, wkv[:, 512:]).astype(BF16)
        yield
        wrapped = jnp.where((lat == 0) & (wr == 0), 2, 0)
        for g, levels in enumerate(GROUPS):
            at = pl.ds(g * GRP, GRP)
            for _ in attention(q.at[at], k.at[at], v.at[at], bias[wrapped + g], att, levels, 0, POS, POS):
                yield
        a = (aft[...].astype(F32) + mm(gather(att, slice(None)), wo[...])).astype(BF16)
        yield
        done[...] = a

    def back_half(w):
        wr, wc_ = 1 - w // 2, 1 - w % 2
        n = norm(done[...]).astype(BF16)
        yield
        for j in range(0, 2048, 512):
            hid[:, j:j + 512] = gelu(mm(n, w1[:, j:j + 512])).astype(BF16)
            yield
        for j in range(0, 512, 256):
            f = (done[:, j:j + 256].astype(F32) + mm(hid[...], w2[:, j:j + 256])).astype(BF16)
            fs[pl.ds(SR + WR * wr, WR), pl.ds(SC + WC * wc_, WC), :, j:j + 256] = f.reshape(WR, WC, LEV, -1)
            yield

    def window(w, carry):
        for _ in back_half(w - 1):
            pass

        @pl.when(w == 1)
        def _():
            for copy in first[2:4] + second[:3]:
                copy.start()
            first[1].wait_recv()

        @pl.when(w == 2)
        def _():
            second[3].start()
            back[0].start()
            first[0].wait_recv()

        @pl.when(w == 3)
        def _():
            second[4].start()
            back[1].start()
            for copy in first[2:]:
                copy.wait_recv()

        for _ in front(w):
            pass
        return carry

    loaded("bias", "wo")
    for _ in front(0):
        pass
    first[4].start()
    loaded("w1", "w2")
    load("wm", "wc", "cbias", "wco")
    lax.fori_loop(1, 4, window, 0)
    for _ in back_half(3):
        pass
    for copy in back[2:]:
        copy.start()
    keep.start()

    loaded("wm")
    for copy in second:
        copy.wait_recv()
    f = fs[pl.ds(0, rows), pl.ds(0, cols)].reshape(rows // 2, 2, cols // 2, 2, LEV, -1)
    f = [f[:, j % 2, :, j // 2].reshape(WIN, -1) for j in range(4)]
    m = norm(jnp.concatenate(f, axis=1)).astype(BF16)
    for j in range(0, 1024, 512):
        cin[:, j:j + 512] = mm(m, wm[:, j:j + 512]).astype(BF16)
    split_tiles(cnat, norm(cin[...]))
    cnat[:, WIN:] = jnp.zeros_like(cnat[:, WIN:])
    nk = jnp.concatenate([by_level(cnat, levels, 0, POS) for levels in GROUPS], axis=0)
    loaded("wc", "cbias", "wco")
    for j in range(0, 1024, 512):
        ck[:, j:j + 512] = mm(nk, wc[:, 1024 + j:1536 + j]).astype(BF16)
        cv[:, j:j + 512] = mm(nk, wc[:, 2048 + j:2560 + j]).astype(BF16)
    wrapped = jnp.where(lat == 0, 4, 0)
    third = backward(
        cs, coarse, [((3, 6), (6, 12)), ((3, 6), (0, 6)), ((0, 3), (6, 12))], WR, WC, s4, r4
    )
    keep_too = pltpu.make_async_copy(
        part(cs, (0, SR), (0, SC)), part(coarse, (SR, WR), (SC, WC)), own_sem.at[1]
    )
    for half in (0, 1):
        nq = [by_level(cnat, levels, half * POS // 2, QPAD) for levels in GROUPS]
        nq = jnp.concatenate(nq, axis=0)
        for j in range(0, 1024, 512):
            cq[:, j:j + 512] = (mm(nq, wc[:, j:j + 512]) * scale).astype(BF16)
        for g, levels in enumerate(GROUPS):
            at = pl.ds(g * 2 * QPAD, 2 * QPAD)
            keys = pl.ds(g * GRP, GRP)
            for _ in attention(
                cq.at[at], ck.at[keys], cv.at[keys], cbias[wrapped + g * 2 + half],
                catt, levels, half * POS // 2, QPAD, POS // 2,
            ):
                pass
        mixed = gather(catt, slice(half * GRP, (half + 1) * GRP))
        at = slice(half * GRP, (half + 1) * GRP)
        for j in range(0, 1024, 512):
            t = (cin[at, j:j + 512].astype(F32) + mm(mixed, wco[:, j:j + 512])).astype(BF16)
            cs[half * SR:(half + 1) * SR, :, :, j:j + 512] = t.reshape(SR, WC, LEV, -1)
        if half == 0:
            third[0].start()
            third[1].start()
        else:
            third[2].start()
            keep_too.start()
    for copy in back + third:
        copy.wait_recv()
    keep.wait()
    keep_too.wait()
    for copy in first + second + back + third:
        copy.wait_send()


def local(
    n_lat, n_lon, tokens, surface_kind, kind_table, attn_q_w, attn_kv_w, attn_out_w,
    mlp_in_w, mlp_out_w, merge_w, coarse_qkv_w, coarse_out_w,
):
    rows, cols, lev, width = tokens.shape
    consts = [jnp.asarray(a) for a in biases()]
    weights = [attn_q_w, attn_kv_w, attn_out_w, mlp_in_w, mlp_out_w, merge_w, coarse_qkv_w, coarse_out_w]
    hbm = pl.BlockSpec(memory_space=pl.ANY)
    dma = pltpu.SemaphoreType.DMA
    buf = lambda *shape: pltpu.VMEM(shape, BF16)
    frame = buf(rows + SR, cols + SC, lev, width)
    return pl.pallas_call(
        functools.partial(kernel, n_lat, n_lon),
        out_shape=(
            buf(rows, cols, lev, width),
            buf(rows // 2, cols // 2, lev, 2 * width),
        ),
        in_specs=[hbm] * 13,
        out_specs=(hbm, hbm),
        scratch_shapes=[
            *[pltpu.VMEM(a.shape, a.dtype) for a in [surface_kind, kind_table] + consts + weights],
            frame, frame, *[buf(WIN, width)] * 3, *[pltpu.VMEM((width // LANES, WIN, LANES), F32)] * 2,
            buf(WIN, width), buf(WIN, width),
            buf(WIN, 4 * width),
            buf(WIN, 2 * width), buf(4 * QPAD, 2 * width), buf(WIN, 2 * width), buf(WIN, 2 * width),
            pltpu.VMEM((2 * width // LANES, WIN + LEV * (2 * QPAD - POS), LANES), F32),
            pltpu.VMEM((2 * width // LANES, WIN + LEV * (2 * QPAD - POS), LANES), F32),
            buf(WR, WC, lev, 2 * width),
            dma((13,)), dma((2,)), dma((5,)), dma((5,)), dma((5,)), dma((5,)), dma((5,)), dma((5,)),
            dma((3,)), dma((3,)),
        ],
        compiler_params=pltpu.CompilerParams(
            collective_id=0, has_side_effects=True, vmem_limit_bytes=60 * 1024 * 1024
        ),
        name="block",
    )(tokens, surface_kind, kind_table, *consts, *weights)


def solution(mesh):
    grid = P("lat", "lon", None, None)
    return jax.shard_map(
        functools.partial(local, mesh.shape["lat"], mesh.shape["lon"]),
        mesh=mesh,
        in_specs=(grid, P("lat", "lon")) + (P(),) * 9,
        out_specs=(grid, grid),
        check_vma=False,
    )
```
